32 devices in a mesh: fsdp: 8 (over y, x, core), seq: 4 (over z).
Axes of the slice: x: 2, y: 2, z: 4, core: 2. Of those that a mesh axis runs over, the one named last changes fastest.
Arguments:
- hidden: bfloat16 [4096, 5120], P(('fsdp', 'seq')), may hold values from -7 to 7
- destination: int32 [4096], P(('fsdp', 'seq')), may hold values from 0 to 4095, as said below
- segment_ids: int32 [8, 512], P('fsdp'), may hold values from 0 to 7, never falling along the last dimension, each value on 1 to 256 neighbouring positions
- cotangent: bfloat16 [4096, 5120], P('fsdp', 'seq'), may hold values from -6 to 6
- w_query: bfloat16 [5120, 5120], P('fsdp', 'seq'), may hold values from -0.078125 to 0.078125
- key_weight: bfloat16 [5120, 1024], P('fsdp', 'seq'), may hold values from -0.078125 to 0.078125
- value_weight: bfloat16 [5120, 1024], P('fsdp', 'seq'), may hold values from -0.078125 to 0.078125
Outputs:
- attn_out: bfloat16 [4096, 5120], P('fsdp', 'seq')
- grad_query: float32 [5120, 5120], P('fsdp', 'seq')
- grad_key: float32 [5120, 1024], P('fsdp', 'seq')
- grad_value: float32 [5120, 1024], P('fsdp', 'seq')
The draws below stay inside these ranges and needn't reach their ends.
Inputs may be any that keep to these rules, and one draw needn't show every extreme that they name: destination is a permutation of the 4096 packed positions (pack * 512 + position in the pack); with packed rows laid 128 to a device in order, the 128 rows of one device go to exactly 16 devices, 8 rows to each.
All inputs are finite; a program needn't handle non-finite values.
Results may differ from the reference program's by a relative error of at most 0.025.
The reference program's roundings to bfloat16 on the way count: a program that leaves them out, or rounds other values in their place, can miss the bound.
Values may be sent and summed in bfloat16 or wider, within the bound.
No kernel may reach another device: no remote copies, remote signals or barrier semaphores. Data moves between devices by JAX's collectives and lax.ppermute only.
A program may use at most 128 MiB of HBM per device.

```python
import math
import jax
import jax.numpy as jnp
import numpy as np
from jax import lax

MODEL_WIDTH = 5120
HQ = 40
KEY_VALUE_HEADS = 8
HEAD_DIMENSION = 128
TOK_DEV = 128
RESP = 8
PACK = 512
TOKENS = 4096
CAP = 8
MAXLEN = 256
N_FSDP = 8
N_SEQ = 4


def draw_hidden(key, part):
    key = jax.random.fold_in(key, 5)
    first = jax.random.fold_in(key, 0)
    values = jnp.clip(jax.random.normal(first, (TOKENS, MODEL_WIDTH), jnp.float32), -6.0, 6.0)
    return values.astype(jnp.bfloat16)


def draw_destination(key, part):
    key = jax.random.fold_in(key, 11)
    n_dev = N_FSDP * N_SEQ
    keys = jax.random.split(key, 4)
    sigma = jax.random.permutation(keys[0], n_dev)
    tau = jax.random.permutation(keys[1], n_dev)
    row_perm = jax.vmap(lambda k: jax.random.permutation(k, TOK_DEV))(jax.random.split(keys[2], n_dev))
    slot_perm = jax.vmap(lambda k: jax.random.permutation(k, TOK_DEV))(jax.random.split(keys[3], n_dev))
    source = jnp.arange(n_dev, dtype=jnp.int32)[:, None]
    block = row_perm // CAP
    within = row_perm % CAP
    target = sigma[(tau[source] + block) % n_dev]
    local = slot_perm[target, block * CAP + within]
    return (target * TOK_DEV + local).reshape(-1).astype(jnp.int32)


def shard_levels(key, extent, shards, low, top_value):
    loudness = 1.0
    for dim, blocks in shards:
        heights = jax.random.uniform(jax.random.fold_in(jax.random.fold_in(key, 6), dim), (blocks,), jnp.float32, low / len(shards), top_value / len(shards))
        loudness = loudness * jnp.repeat(jnp.exp(heights), extent[dim] // blocks).reshape((-1,) + (1,) * (len(extent) - 1 - dim))
    return loudness


def length_profile(amount, total, limit, lean):
    loads = [(1 << 20) // math.isqrt(standing ** lean) + 1 for standing in range(2, amount + 1)]
    surplus, counts = total - limit - (amount - 1), [1] * (amount - 1)
    while surplus > 0:
        free = [i for i in range(amount - 1) if counts[i] < limit]
        pool, left = sum([loads[i] for i in free]), surplus
        for i in free:
            extra = min(limit - counts[i], max(1, left * loads[i] // pool), surplus)
            counts[i] = counts[i] + extra
            surplus = surplus - extra
    return np.array([limit] + counts)


def ragged_sizes(key, count, total, bound, slope):
    if count == 2:
        one = jax.random.randint(key, (), max(1, total - bound), min(bound, total - 1) + 1)
        return jnp.stack([one, total - one])
    lengths = jnp.asarray(length_profile(count, total, bound, slope), jnp.int32)
    couples = (count - 1) // 2
    donor, taker = lengths[1:1 + 2 * couples:2], lengths[2:2 + 2 * couples:2]
    slack = jnp.minimum(donor - 1, bound - taker)
    shifted = jax.random.randint(jax.random.fold_in(key, 1), (couples,), 0, 1 << 20) % (slack + 1)
    lengths = lengths.at[1:1 + 2 * couples:2].set(donor - shifted).at[2:2 + 2 * couples:2].set(taker + shifted)
    return lengths[jax.random.permutation(jax.random.fold_in(key, 2), count)]


def gaussian(stream_key, dims, scale, most, cuts=(), held_as=jnp.bfloat16):
    gain = shard_levels(stream_key, dims, cuts, -0.22, 0.18) if cuts else 1.0
    values = jax.random.normal(stream_key, dims, jnp.float32) * scale * gain
    return jnp.minimum(jnp.maximum(values, -most), most).astype(held_as)


def setup_inputs(seed: int = 0) -> dict:
    seeds = jax.random.split(jax.random.key(seed), 8)
    hidden = draw_hidden(jax.random.fold_in(seeds[7], 71), 0)
    destination = draw_destination(jax.random.fold_in(seeds[7], 71), 0)
    segment_ids = jax.vmap(lambda own: jnp.searchsorted(jnp.cumsum(ragged_sizes(own, RESP, PACK, MAXLEN, 2)), jnp.arange(PACK), side="right"))(jax.random.split(seeds[2], N_FSDP)).reshape((N_FSDP, PACK)).astype(jnp.int32)
    cotangent = gaussian(seeds[3], (TOKENS, HQ * HEAD_DIMENSION), 1.0, 6.0, ((0, 8), (1, 4)))
    w_query = gaussian(seeds[4], (MODEL_WIDTH, HQ * HEAD_DIMENSION), MODEL_WIDTH ** -0.5, 0.078125, ((0, 8), (1, 4)))
    key_weight = gaussian(seeds[5], (MODEL_WIDTH, KEY_VALUE_HEADS * HEAD_DIMENSION), MODEL_WIDTH ** -0.5, 0.078125, ((0, 8), (1, 4)))
    value_weight = gaussian(seeds[6], (MODEL_WIDTH, KEY_VALUE_HEADS * HEAD_DIMENSION), MODEL_WIDTH ** -0.5, 0.078125, ((0, 8), (1, 4)))
    return {"hidden": hidden, "destination": destination, "segment_ids": segment_ids, "cotangent": cotangent, "w_query": w_query, "key_weight": key_weight, "value_weight": value_weight}


def attend_heads(query, keys, values, segments, cotangent, head_size):
    length = query.shape[0]
    heads = query.shape[1] // head_size
    groups = heads // (keys.shape[1] // head_size)
    scale = 1.0 / math.sqrt(head_size)
    order = jnp.arange(length, dtype=jnp.int32)
    allowed = (segments[:, None] == segments[None, :]) & (order[None, :] <= order[:, None])

    def one_head(index, carry):
        out_all, dq_all, dk_sum, dv_sum = carry
        start = index * head_size
        kv_start = index // groups * head_size
        q_h = lax.dynamic_slice_in_dim(query, start, head_size, 1)
        k_h = lax.dynamic_slice_in_dim(keys, kv_start, head_size, 1)
        v_h = lax.dynamic_slice_in_dim(values, kv_start, head_size, 1)
        d_h = lax.dynamic_slice_in_dim(cotangent, start, head_size, 1)
        scores = jnp.dot(q_h, k_h.T, preferred_element_type=jnp.float32) * scale
        scores = jnp.where(allowed, scores, -1e+30)
        top = lax.optimization_barrier(jnp.max(scores, axis=1, keepdims=True))
        weights = jnp.exp(scores - top)
        probs = weights / lax.optimization_barrier(jnp.sum(weights, axis=1, keepdims=True))
        probs_b = probs.astype(jnp.bfloat16)
        out_h = jnp.dot(probs_b, v_h, preferred_element_type=jnp.float32).astype(jnp.bfloat16)
        delta = lax.optimization_barrier(jnp.sum(d_h.astype(jnp.float32) * out_h.astype(jnp.float32), axis=1, keepdims=True))
        dv_h = jnp.dot(probs_b.T, d_h, preferred_element_type=jnp.float32)
        dprob = jnp.dot(d_h, v_h.T, preferred_element_type=jnp.float32)
        dscore = (probs * (dprob - delta)).astype(jnp.bfloat16)
        dq_h = (jnp.dot(dscore, k_h, preferred_element_type=jnp.float32) * scale).astype(jnp.bfloat16)
        dk_h = jnp.dot(dscore.T, q_h, preferred_element_type=jnp.float32)
        out_all = lax.dynamic_update_slice_in_dim(out_all, out_h, start, 1)
        dq_all = lax.dynamic_update_slice_in_dim(dq_all, dq_h, start, 1)
        dk_old = lax.dynamic_slice_in_dim(dk_sum, kv_start, head_size, 1)
        dk_sum = lax.dynamic_update_slice_in_dim(dk_sum, dk_old + dk_h, kv_start, 1)
        dv_old = lax.dynamic_slice_in_dim(dv_sum, kv_start, head_size, 1)
        dv_sum = lax.dynamic_update_slice_in_dim(dv_sum, dv_old + dv_h, kv_start, 1)
        return (out_all, dq_all, dk_sum, dv_sum)
    initial_carry = (jnp.zeros(query.shape, jnp.bfloat16), jnp.zeros(query.shape, jnp.bfloat16), jnp.zeros(keys.shape, jnp.float32), jnp.zeros(keys.shape, jnp.float32))
    out_all, dq_all, dk_sum, dv_sum = lax.fori_loop(0, heads, one_head, initial_carry)
    return (out_all, dq_all, (dk_sum * scale).astype(jnp.bfloat16), dv_sum.astype(jnp.bfloat16))

def reference(hidden, destination, segment_ids, cotangent, w_query, key_weight, value_weight):
    packed = jnp.zeros_like(hidden).at[destination].set(hidden)
    query = jnp.dot(packed, w_query, preferred_element_type=jnp.float32).astype(jnp.bfloat16)
    keys = jnp.dot(packed, key_weight, preferred_element_type=jnp.float32).astype(jnp.bfloat16)
    values = jnp.dot(packed, value_weight, preferred_element_type=jnp.float32).astype(jnp.bfloat16)
    packs = segment_ids.shape[0]

    def one_pack(items):
        q_p, k_p, v_p, s_p, c_p = items
        return attend_heads(q_p, k_p, v_p, s_p, c_p, HEAD_DIMENSION)
    out_all, dq_all, dk_all, dv_all = lax.map(one_pack, (query.reshape(packs, PACK, query.shape[1]), keys.reshape(packs, PACK, keys.shape[1]), values.reshape(packs, PACK, values.shape[1]), segment_ids, cotangent.reshape(packs, PACK, cotangent.shape[1])))
    cols_q = query.shape[1]
    cols_k = keys.shape[1]
    joined = jnp.concatenate([dq_all.reshape(-1, cols_q), dk_all.reshape(-1, cols_k), dv_all.reshape(-1, cols_k)], axis=1)
    grads = lax.dot_general(packed, joined, (((0,), (0,)), ((), ())), preferred_element_type=jnp.float32)
    return (out_all.reshape(-1, cols_q), grads[:, :cols_q], grads[:, cols_q:cols_q + cols_k], grads[:, cols_q + cols_k:])
```

```python
import functools
import math

import jax
import jax.numpy as jnp
from jax import lax
from jax.experimental import pallas as pl
from jax.experimental.pallas import tpu as pltpu
from jax.sharding import PartitionSpec as P

HEAD_DIMENSION = 128
VMEM_LIMIT = 56 * 1024 * 1024
ANY = pl.BlockSpec(memory_space=pl.ANY)
SMEM = pl.BlockSpec(memory_space=pltpu.SMEM)
VMEM = pl.BlockSpec(memory_space=pltpu.VMEM)


def swap(x, axis, bit):
    n = lax.axis_size(axis)
    return lax.ppermute(x, axis, [(i, i ^ bit) for i in range(n)])


def after(x, *others):
    return lax.optimization_barrier((x, *others))[0] if others else x


def together(*groups):
    flat = lax.optimization_barrier(tuple(x for group in groups for x in group))
    out, at = [], 0
    for group in groups:
        out.append(list(flat[at : at + len(group)]))
        at += len(group)
    return out


def spread(chunk, bits):
    have = {0: chunk}
    for bit in bits:
        for m in sorted(have):
            have[m ^ bit] = swap(have[m], "fsdp", bit)
    return [have[m] for m in range(len(have))]


def axis_bits(n):
    return [1 << i for i in range(1, n.bit_length() - 1)]


def gather_step(x, axis, bit):
    other = swap(x, axis, bit)
    mine_first = (lax.axis_index(axis) & bit) == 0
    return jnp.where(mine_first, jnp.concatenate([x, other]), jnp.concatenate([other, x]))


def line_step(up, down):
    n = lax.axis_size("seq")
    return (
        lax.ppermute(up, "seq", [(i, i + 1) for i in range(n - 1)]),
        lax.ppermute(down, "seq", [(i + 1, i) for i in range(n - 1)]),
    )


def line_gather(x):
    up, down = [x], [x]
    for _ in range(1, lax.axis_size("seq")):
        u, d = line_step(up[-1], down[-1])
        up.append(u)
        down.append(d)
    return up[1:], down[1:]


def gather_all(blocks, rows, short):
    n_fsdp, n_seq = lax.axis_size("fsdp"), lax.axis_size("seq")
    high = axis_bits(n_fsdp)
    short = short[None]
    if len(high) != 2 or n_seq != 4 or len(blocks) != 2:
        weights = [spread(block, high + [1]) for block in blocks]
        up, down = line_gather(rows)
        bit = 1
        while bit < n_seq:
            short = gather_step(short, "seq", bit)
            bit *= 2
        short = short[None]
        bit = 1
        while bit < n_fsdp:
            short = gather_step(short, "fsdp", bit)
            bit *= 2
        return weights, up, down, short, short[lax.axis_index("fsdp")]
    x, y = high
    p, q = blocks
    p_x, q_y = swap(p, "fsdp", x), swap(q, "fsdp", y)
    up1, down1 = line_step(rows, rows)
    short1 = gather_step(short, "seq", 1)
    (p, q, p_x, q_y, up1, down1, short1), = together((p, q, p_x, q_y, up1, down1, short1))
    p_y, q_x = swap(p, "fsdp", y), swap(q, "fsdp", x)
    up2, down2 = line_step(up1, down1)
    short2 = gather_step(short1, "seq", 2)
    p_c, q_c = swap(p, "fsdp", 1), swap(q, "fsdp", 1)
    p_xc, q_yc = swap(p_x, "fsdp", 1), swap(q_y, "fsdp", 1)
    (p_x, q_y, p_y, q_x, up2, down2, short2, p_c, q_c, p_xc, q_yc), = together(
        (p_x, q_y, p_y, q_x, up2, down2, short2, p_c, q_c, p_xc, q_yc)
    )
    p_xy, q_xy = swap(p_x, "fsdp", y), swap(q_y, "fsdp", x)
    up3, down3 = line_step(up2, down2)
    p_yc, q_xc = swap(p_y, "fsdp", 1), swap(q_x, "fsdp", 1)
    short3 = gather_step(short2[None], "fsdp", 1)
    (p_xy, q_xy, up3, down3, p_yc, q_xc, short3), = together(
        (p_xy, q_xy, up3, down3, p_yc, q_xc, short3)
    )
    p_xyc, q_xyc = swap(p_xy, "fsdp", 1), swap(q_xy, "fsdp", 1)
    short4 = gather_step(gather_step(short3, "fsdp", x), "fsdp", y)
    weights = [
        [p, p_c, p_x, p_xc, p_y, p_yc, p_xy, p_xyc],
        [q, q_c, q_x, q_xc, q_y, q_yc, q_xy, q_xyc],
    ]
    return weights, [up1, up2, up3], [down1, down2, down3], short4, short2


def gather_plane(block):
    n = lax.axis_size("fsdp")
    high = axis_bits(n)
    if len(high) != 2:
        return [[(0, part)] for part in spread(block, high + [1])]
    x, y = high
    half = block.shape[0] // 2
    from_x, from_y = swap(block, "fsdp", x), swap(block, "fsdp", y)
    top, bottom = swap(from_x[:half], "fsdp", y), swap(from_y[half:], "fsdp", x)
    whole = [(0, block)], [(0, from_x)], [(0, from_y)], [(0, top), (half, bottom)]
    out = []
    for parts in whole:
        out.append(parts)
        out.append([(at, swap(part, "fsdp", 1)) for at, part in parts])
    return out


def line_pick(x, up, down):
    n = lax.axis_size("seq")
    z = lax.axis_index("seq")
    return [x] + [jnp.where(z + k < n, down[k - 1], up[n - k - 1]) for k in range(1, n)]


def project_kernel(n_seq, n_fsdp, cap, me_ref, slot_ref, *refs):
    own = refs[0]
    up = refs[1:n_seq]
    down = refs[n_seq : 2 * n_seq - 1]
    chunks = refs[2 * n_seq - 1 : 2 * n_seq - 1 + n_fsdp]
    out_ref, a_v, w_v, acc, sem_a, sem_w = refs[2 * n_seq - 1 + n_fsdp :]
    me, z = me_ref[0], me_ref[1]
    tok = own.shape[0]
    depth = chunks[0].shape[0]
    in_w = []
    for m in range(n_fsdp):
        start = pl.multiple_of((me ^ m) * depth, depth)
        in_w.append(pltpu.make_async_copy(chunks[m], w_v.at[pl.ds(start, depth)], sem_w.at[m]))
    in_rows = [pltpu.make_async_copy(own, a_v.at[pl.ds(0, tok)], sem_a.at[0])]
    in_rows[0].start()
    for k in range(1, n_seq):
        spot = a_v.at[pl.ds(k * tok, tok)]
        below = pltpu.make_async_copy(up[n_seq - k - 1], spot, sem_a.at[k])
        above = pltpu.make_async_copy(down[k - 1], spot, sem_a.at[k])
        pl.when(z + k < n_seq)(above.start)
        pl.when(z + k >= n_seq)(below.start)
        in_rows.append(above)
    for copy in in_w:
        copy.start()
    for copy in in_rows:
        copy.wait()
    for j in range(n_fsdp // 2):
        in_w[2 * j].wait()
        in_w[2 * j + 1].wait()
        start = pl.multiple_of(((me >> 1) ^ j) * (2 * depth), 2 * depth)
        part = jnp.dot(
            a_v[:, pl.ds(start, 2 * depth)],
            w_v[pl.ds(start, 2 * depth), :],
            preferred_element_type=jnp.float32,
        )
        if j == 0:
            acc[...] = part
        else:
            acc[...] += part
    qkv = acc[...].astype(jnp.bfloat16)
    slot = slot_ref[...]
    order = lax.broadcasted_iota(jnp.int32, (n_fsdp * cap, slot.shape[1]), 0)
    pick = (slot == order).astype(jnp.bfloat16)
    out_ref[...] = jnp.dot(pick, qkv, preferred_element_type=jnp.float32).astype(jnp.bfloat16)


def project(place, slot, own, up, down, chunks, cap):
    n_seq, n_fsdp = len(up) + 1, len(chunks)
    tok, width = own.shape
    cols = chunks[0].shape[1]
    length = n_seq * tok
    return pl.pallas_call(
        functools.partial(project_kernel, n_seq, n_fsdp, cap),
        out_shape=jax.ShapeDtypeStruct((n_fsdp * cap, cols), jnp.bfloat16),
        in_specs=[SMEM, VMEM] + [ANY] * (2 * n_seq - 1 + n_fsdp),
        out_specs=VMEM,
        scratch_shapes=[
            pltpu.VMEM((length, width), jnp.bfloat16),
            pltpu.VMEM((width, cols), jnp.bfloat16),
            pltpu.VMEM((length, cols), jnp.float32),
            pltpu.SemaphoreType.DMA((n_seq,)),
            pltpu.SemaphoreType.DMA((n_fsdp,)),
        ],
        compiler_params=pltpu.CompilerParams(vmem_limit_bytes=VMEM_LIMIT),
        cost_estimate=pl.CostEstimate(
            flops=2 * length * width * cols + 2 * n_fsdp * cap * length * cols,
            bytes_accessed=2 * (length * width + width * cols + n_fsdp * cap * cols),
            transcendentals=0,
        ),
        name="project",
    )(place, slot, own, *up, *down, *chunks)


def attend_kernel(heads, block, place_ref, seg_row, seg_col, cot_ref, in_ref, *refs):
    out_ref, grad_ref, qkv, bias, dk_sum, dv_sum = refs
    size = HEAD_DIMENSION
    length = qkv.shape[0]
    scale = 1.0 / math.sqrt(size)
    key_pos = lax.broadcasted_iota(jnp.int32, (length, length), 0)
    query_pos = lax.broadcasted_iota(jnp.int32, (length, length), 1)
    allowed = (seg_col[...] == seg_row[...]) & (key_pos <= query_pos)
    bias[...] = jnp.where(allowed, 0.0, -1e30)
    spots = lax.broadcasted_iota(jnp.int32, (length, in_ref.shape[0]), 0)
    pick = (spots == place_ref[...]).astype(jnp.bfloat16)
    qkv[...] = jnp.dot(pick, in_ref[...], preferred_element_type=jnp.float32).astype(jnp.bfloat16)
    keys = qkv[:, heads * size : (heads + 1) * size]
    values = qkv[:, (heads + 1) * size : (heads + 2) * size]
    keys_t = keys.T
    values_t = values.T
    dk_sum[...] = jnp.zeros_like(dk_sum)
    dv_sum[...] = jnp.zeros_like(dv_sum)
    for h in range(heads):
        q_h = qkv[:, h * size : (h + 1) * size]
        d_h = cot_ref[:, h * size : (h + 1) * size]
        q_t = q_h.T
        d_t = d_h.T
        for start in range(0, length, block):
            stop = start + block
            scores = jnp.dot(keys[:stop], q_t[:, start:stop], preferred_element_type=jnp.float32)
            scores = scores + bias[:stop, start:stop]
            top = jnp.max(scores, axis=0, keepdims=True)
            weights = jnp.exp2((scores - top) * (scale * math.log2(math.e)))
            probs = weights * (1.0 / jnp.sum(weights, axis=0, keepdims=True))
            probs_b = probs.astype(jnp.bfloat16)
            out_t = jnp.dot(values_t[:, :stop], probs_b, preferred_element_type=jnp.float32).astype(
                jnp.bfloat16
            )
            delta = jnp.sum(
                d_t[:, start:stop].astype(jnp.float32) * out_t.astype(jnp.float32), axis=0, keepdims=True
            )
            dprob = jnp.dot(values[:stop], d_t[:, start:stop], preferred_element_type=jnp.float32)
            dscore = (probs * (dprob - delta)).astype(jnp.bfloat16)
            dq_t = (
                jnp.dot(keys_t[:, :stop], dscore, preferred_element_type=jnp.float32) * scale
            ).astype(jnp.bfloat16)
            dk_sum[:stop] += jnp.dot(dscore, q_h[start:stop], preferred_element_type=jnp.float32)
            dv_sum[:stop] += jnp.dot(probs_b, d_h[start:stop], preferred_element_type=jnp.float32)
            out_ref[start:stop, h * size : (h + 1) * size] = out_t.T
            grad_ref[start:stop, h * size : (h + 1) * size] = dq_t.T
    grad_ref[:, heads * size : (heads + 1) * size] = (dk_sum[...] * scale).astype(jnp.bfloat16)
    grad_ref[:, (heads + 1) * size : (heads + 2) * size] = dv_sum[...].astype(jnp.bfloat16)


def attend(place, segments, cotangent, group, arrived):
    slots, cols = arrived.shape
    size = HEAD_DIMENSION
    heads = cols // size - 2
    length = cotangent.shape[0]
    return pl.pallas_call(
        functools.partial(attend_kernel, heads, 256),
        grid=(1,),
        out_shape=[
            jax.ShapeDtypeStruct((length, heads * size), jnp.bfloat16),
            jax.ShapeDtypeStruct((length, cols), jnp.bfloat16),
        ],
        in_specs=[VMEM, VMEM, VMEM, pl.BlockSpec((length, heads * size), lambda i: (0, group)), VMEM],
        out_specs=[VMEM, VMEM],
        scratch_shapes=[
            pltpu.VMEM((length, cols), jnp.bfloat16),
            pltpu.VMEM((length, length), jnp.float32),
            pltpu.VMEM((length, size), jnp.float32),
            pltpu.VMEM((length, size), jnp.float32),
        ],
        compiler_params=pltpu.CompilerParams(vmem_limit_bytes=VMEM_LIMIT),
        cost_estimate=pl.CostEstimate(
            flops=12 * heads * length * length * size + 2 * length * slots * cols,
            bytes_accessed=2 * (slots * cols + 3 * length * cols),
            transcendentals=heads * length * length,
        ),
        name="attend",
    )(place, segments[None, :], segments[:, None], cotangent, arrived)


def pack_kernel(count, length, has_before, *refs):
    rows, spots = refs[:count], refs[count : 2 * count]
    out_ref = refs[-1]
    base = pl.program_id(0) * length
    order = lax.broadcasted_iota(jnp.int32, (rows[0].shape[1], length), 1) + base
    total = refs[2 * count][...].astype(jnp.float32) if has_before else None
    for k in range(count):
        pick = (order == spots[k][...]).astype(jnp.bfloat16)
        part = jnp.dot(rows[k][...], pick, preferred_element_type=jnp.float32)
        total = part if total is None else total + part
    out_ref[...] = total.astype(jnp.bfloat16)


def pack_columns(rows, spots, tokens, length, before):
    count = len(rows)
    cols, each = rows[0].shape
    extra = [] if before is None else [before]
    block = pl.BlockSpec((cols, length), lambda i: (0, i))
    return pl.pallas_call(
        functools.partial(pack_kernel, count, length, before is not None),
        grid=(tokens // length,),
        out_shape=jax.ShapeDtypeStruct((cols, tokens), jnp.bfloat16),
        in_specs=[pl.BlockSpec((cols, each), lambda i: (0, 0))] * count
        + [pl.BlockSpec((each, 1), lambda i: (0, 0))] * count
        + [block] * len(extra),
        out_specs=block,
        compiler_params=pltpu.CompilerParams(vmem_limit_bytes=VMEM_LIMIT),
        cost_estimate=pl.CostEstimate(
            flops=2 * tokens * each * count * cols,
            bytes_accessed=4 * tokens * cols,
            transcendentals=0,
        ),
        name="pack_columns",
    )(*rows, *spots, *extra)


def grads_kernel(layout, group, aliased, me_ref, packed_ref, *refs):
    count = sum(len(parts) for parts in layout)
    gq_ref, gk_ref, gv_ref, d_v, acc, sem, sem_o = refs[count + (3 if aliased else 0) :]
    me = me_ref[0]
    length = packed_ref.shape[1] // len(layout)
    cols = d_v.shape[1]
    size = HEAD_DIMENSION
    copies = []
    at = 0
    for m, parts in enumerate(layout):
        copies.append([])
        for offset, rows in parts:
            start = pl.multiple_of((me ^ m) * length + offset, rows)
            copies[m].append(
                pltpu.make_async_copy(refs[at], d_v.at[pl.ds(start, rows)], sem.at[at])
            )
            copies[m][-1].start()
            at += 1
    for j in range(len(layout) // 2):
        for copy in copies[2 * j] + copies[2 * j + 1]:
            copy.wait()
        start = pl.multiple_of(((me >> 1) ^ j) * (2 * length), 2 * length)
        part = jnp.dot(
            packed_ref[:, pl.ds(start, 2 * length)],
            d_v[pl.ds(start, 2 * length), :],
            preferred_element_type=jnp.float32,
        )
        if j == 0:
            acc[...] = part
        else:
            acc[...] += part
    q_cols = cols - 2 * size
    outs = (
        pltpu.make_async_copy(
            acc.at[:, pl.ds(0, q_cols)], gq_ref.at[:, pl.ds(group * q_cols, q_cols)], sem_o.at[0]
        ),
        pltpu.make_async_copy(
            acc.at[:, pl.ds(q_cols, size)], gk_ref.at[:, pl.ds(group * size, size)], sem_o.at[1]
        ),
        pltpu.make_async_copy(
            acc.at[:, pl.ds(q_cols + size, size)], gv_ref.at[:, pl.ds(group * size, size)], sem_o.at[2]
        ),
    )
    for copy in outs:
        copy.start()
    for copy in outs:
        copy.wait()


def gradients(place, packed, chunks, group, groups, before):
    layout = [[(at, part.shape[0]) for at, part in parts] for parts in chunks]
    pieces = [part for parts in chunks for _, part in parts]
    width, tokens = packed.shape
    cols = pieces[0].shape[1]
    size = HEAD_DIMENSION
    shapes = [
        jax.ShapeDtypeStruct((width, groups * (cols - 2 * size)), jnp.float32),
        jax.ShapeDtypeStruct((width, groups * size), jnp.float32),
        jax.ShapeDtypeStruct((width, groups * size), jnp.float32),
    ]
    extra = [] if before is None else list(before)
    return pl.pallas_call(
        functools.partial(grads_kernel, layout, group, before is not None),
        out_shape=shapes,
        in_specs=[SMEM, VMEM] + [ANY] * (len(pieces) + len(extra)),
        out_specs=[ANY] * 3,
        input_output_aliases={2 + len(pieces) + i: i for i in range(len(extra))},
        scratch_shapes=[
            pltpu.VMEM((tokens, cols), jnp.bfloat16),
            pltpu.VMEM((width, cols), jnp.float32),
            pltpu.SemaphoreType.DMA((len(pieces),)),
            pltpu.SemaphoreType.DMA((3,)),
        ],
        compiler_params=pltpu.CompilerParams(vmem_limit_bytes=VMEM_LIMIT),
        cost_estimate=pl.CostEstimate(
            flops=2 * tokens * width * cols,
            bytes_accessed=2 * tokens * (width + cols) + 4 * width * cols,
            transcendentals=0,
        ),
        name="gradients",
    )(place, packed, *pieces, *extra)


def on_device(hidden, destination, segment_ids, cotangent, w_query, key_weight, value_weight):
    tok_rows, width = hidden.shape
    n_fsdp = lax.axis_size("fsdp")
    n_seq = lax.axis_size("seq")
    length = n_seq * tok_rows
    size = HEAD_DIMENSION
    groups = key_weight.shape[1] // size
    q_cols = w_query.shape[1] // groups
    cap = n_seq * n_seq * (2 * tok_rows // (n_fsdp * n_seq))
    f = lax.axis_index("fsdp")
    z = lax.axis_index("seq")
    here = jnp.stack([f, z]).astype(jnp.int32)

    blocks = [
        jnp.concatenate(
            [
                w_query[:, g * q_cols : (g + 1) * q_cols],
                key_weight[:, g * size : (g + 1) * size],
                value_weight[:, g * size : (g + 1) * size],
            ],
            axis=1,
        )
        for g in range(groups)
    ]
    weights, up, down, dest, mine = gather_all(blocks, hidden, destination)

    mine = mine.reshape(length)
    target = mine // length
    order = jnp.arange(length, dtype=jnp.int32)
    earlier = (target[:, None] == target[None, :]) & (order[:, None] < order[None, :])
    rank = jnp.sum(earlier.astype(jnp.int32), axis=0)
    slot = (target * cap + rank).reshape(n_seq, tok_rows)
    slot = lax.dynamic_slice_in_dim(jnp.concatenate([slot, slot], 0), z, n_seq, 0).reshape(1, length)
    blocks = dest.reshape(n_fsdp, length)
    coming = (blocks // length) == f
    before = (order[:, None] < order[None, :]).astype(jnp.bfloat16)
    rank_in = jnp.dot(coming.astype(jnp.bfloat16), before, preferred_element_type=jnp.float32)
    rank_in = rank_in.astype(jnp.int32)
    nth = jnp.arange(cap, dtype=jnp.int32)
    hit = coming[:, None, :] & (rank_in[:, None, :] == nth[None, :, None])
    place = jnp.sum(jnp.where(hit, (blocks % length + 1)[:, None, :], 0), axis=2) - 1
    place = place.reshape(1, n_fsdp * cap)

    columns = lax.all_to_all(
        after(hidden, weights[-1][-2]), "fsdp", split_axis=1, concat_axis=0, tiled=True
    ).T
    c_up, c_down = line_gather(columns)
    columns = line_pick(columns, c_up, c_down)
    twice = jnp.concatenate([dest, dest], axis=1)
    spots = [
        lax.dynamic_index_in_dim(twice, z + k, 1, keepdims=False).reshape(n_fsdp * tok_rows, 1)
        for k in range(n_seq)
    ]
    half = n_seq // 2
    tokens = n_fsdp * length

    arrived = []
    for g in range(groups):
        slots = project(here, slot, hidden, up, down, weights[g], cap)
        arrived.append(lax.all_to_all(slots, "fsdp", split_axis=0, concat_axis=0, tiled=True))

    packed = pack_columns(columns[:half], spots[:half], tokens, length, None)
    arrived[-1] = after(arrived[-1], packed)
    outs, d_chunks = [], []
    for g in range(groups):
        out_g, grad_g = attend(place, segment_ids[0], cotangent, g, arrived[g])
        outs.append(out_g)
        d_chunks.append(gather_plane(grad_g))
    packed = pack_columns(columns[half:], spots[half:], tokens, length, packed)
    grads = None
    for g in range(groups):
        grads = gradients(here, packed, d_chunks[g], g, groups, grads)
    attn_out = jnp.concatenate(outs, axis=1) if groups > 1 else outs[0]
    return (attn_out, *grads)


def solution(mesh):
    placed = (
        P(("fsdp", "seq"), None),
        P(("fsdp", "seq")),
        P("fsdp", None),
        P("fsdp", "seq"),
        P("fsdp", "seq"),
        P("fsdp", "seq"),
        P("fsdp", "seq"),
    )
    return jax.shard_map(
        on_device,
        mesh=mesh,
        in_specs=placed,
        out_specs=(P("fsdp", "seq"), P("fsdp", "seq"), P("fsdp", "seq"), P("fsdp", "seq")),
        check_vma=False,
    )
```

```python
import functools
import math

import jax
import jax.numpy as jnp
from jax import lax
from jax.experimental import pallas as pl
from jax.experimental.pallas import tpu as pltpu
from jax.sharding import PartitionSpec as P

HEAD_DIMENSION = 128
VMEM_LIMIT = 56 * 1024 * 1024
ANY = pl.BlockSpec(memory_space=pl.ANY)
SMEM = pl.BlockSpec(memory_space=pltpu.SMEM)
VMEM = pl.BlockSpec(memory_space=pltpu.VMEM)


def swap(x, axis, bit):
    n = lax.axis_size(axis)
    return lax.ppermute(x, axis, [(i, i ^ bit) for i in range(n)])


def after(x, *others):
    return lax.optimization_barrier((x, *others))[0] if others else x


def together(*groups):
    flat = lax.optimization_barrier(tuple(x for group in groups for x in group))
    out, at = [], 0
    for group in groups:
        out.append(list(flat[at : at + len(group)]))
        at += len(group)
    return out


def spread(chunk, bits):
    have = {0: chunk}
    for bit in bits:
        for m in sorted(have):
            have[m ^ bit] = swap(have[m], "fsdp", bit)
    return [have[m] for m in range(len(have))]


def axis_bits(n):
    return [1 << i for i in range(1, n.bit_length() - 1)]


def line_step(a, b):
    n_fsdp, n = lax.axis_size("fsdp"), lax.axis_size("seq")

    def pairs(up):
        out = []
        for i in range(n_fsdp):
            for z in range(n):
                to = z + (1 if (i & 1) == up else -1)
                out.append((i * n + z, i * n + to if 0 <= to < n else (i ^ 1) * n + z))
        return out

    return lax.ppermute(a, ("fsdp", "seq"), pairs(0)), lax.ppermute(b, ("fsdp", "seq"), pairs(1))


def line_gather(x):
    a, b = [x], [x]
    for _ in range(1, lax.axis_size("seq")):
        a_next, b_next = line_step(a[-1], b[-1])
        a.append(a_next)
        b.append(b_next)
    return a[1:], b[1:]


def everywhere(x):
    n_fsdp, n_seq = lax.axis_size("fsdp"), lax.axis_size("seq")
    sent = jnp.broadcast_to(x, (n_fsdp * n_seq, *x.shape))
    got = lax.all_to_all(sent, ("fsdp", "seq"), split_axis=0, concat_axis=0, tiled=True)
    return got.reshape(n_fsdp, n_seq, *x.shape)


def by_core(x, even, odd):
    n = lax.axis_size("fsdp")
    return lax.ppermute(x, "fsdp", [(i, i ^ (odd if i & 1 else even)) for i in range(n)])


def in_masks(have):
    return [(j, 0, [(0, have[2 * j]), (1, have[2 * j + 1])]) for j in range(len(have) // 2)]


def in_pairs(own, near, far, diagonal):
    return [
        (0, 0, [(0, own[0]), (1, own[1])]),
        (1, 1, [(0, near[0]), (1, near[1])]),
        (2, -1, [(1, far[0]), (0, far[1])]),
        (3, 0, [(0, diagonal[0]), (1, diagonal[1])]),
    ]


def exchange_columns(blocks):
    return lax.all_to_all(blocks, "fsdp", split_axis=0, concat_axis=0, tiled=True)


def gather_all(block, rows, short, columns):
    high = axis_bits(lax.axis_size("fsdp"))
    weights = in_masks(spread(block, high + [1]))
    rows_a, rows_b = line_gather(rows)
    short = everywhere(short)
    return weights, rows_a, rows_b, short, exchange_columns(columns)


def gather_all_rounds(block, rows, short, columns):
    x, y = axis_bits(lax.axis_size("fsdp"))
    a1, b1 = line_step(rows, rows)
    near = [by_core(block, x, y)]
    sibling = swap(block, "fsdp", 1)
    ((a1, b1, *near, sibling, columns),) = together((a1, b1, *near, sibling, columns))
    near.append(by_core(sibling, x, y))
    columns = exchange_columns(columns)
    a2, b2 = line_step(a1, b1)
    ((a2, b2, *near, short, columns),) = together((a2, b2, *near, short, columns))
    diagonal = by_core(near[0], y, x)
    a3, b3 = line_step(a2, b2)
    far = [swap(part, "fsdp", 1) for part in near]
    short = everywhere(short)
    ((a3, b3, diagonal, *far, short, columns),) = together((a3, b3, diagonal, *far, short, columns))
    weights = in_pairs([block, sibling], near, far, [diagonal, swap(diagonal, "fsdp", 1)])
    return weights, [a1, a2, a3], [b1, b2, b3], short, columns


def line_copy(own, a, b, k, z, odd, view, spot, sem):
    if k == 0:
        copy = pltpu.make_async_copy(view(own), spot, sem)
        return copy.start, copy.wait
    n = len(a) + 1
    above = [pltpu.make_async_copy(view(r[k - 1]), spot, sem) for r in (b, a)]
    below = [pltpu.make_async_copy(view(r[n - k - 1]), spot, sem) for r in (a, b)]

    def start():
        for i in range(2):
            pl.when((z + k < n) & (odd == i))(above[i].start)
            pl.when((z + k >= n) & (odd == i))(below[i].start)

    return start, above[0].wait


def project_kernel(n_seq, layout, cap, group, me_ref, slot_ref, *refs):
    own = refs[0]
    rows_a = refs[1:n_seq]
    rows_b = refs[n_seq : 2 * n_seq - 1]
    count = sum(len(flips) for _, _, flips in layout)
    chunks = refs[2 * n_seq - 1 : 2 * n_seq - 1 + count]
    out_ref, a_v, w_v, acc, sem_a, sem_w = refs[2 * n_seq - 1 + count :]
    me, z = me_ref[0], me_ref[1]
    tok = own.shape[0]
    pairs, both, cols = w_v.shape
    depth = both // 2
    steps = []
    at = 0
    for j, (mask, change, flips) in enumerate(layout):
        pair = (me >> 1) ^ (mask + change * (me & 1))
        columns = pl.ds(pl.multiple_of(pair * both, both), both)
        copies = []
        for k in range(n_seq):
            spot = a_v.at[j, pl.ds(k * tok, tok)]
            copies.append(
                line_copy(own, rows_a, rows_b, k, z, me & 1, lambda r, c=columns: r.at[:, c], spot, sem_a.at[j, k])
            )
        for flip in flips:
            start = pl.multiple_of(((me & 1) ^ flip) * depth, depth)
            copy = pltpu.make_async_copy(
                chunks[at].at[:, pl.ds(group * cols, cols)], w_v.at[j, pl.ds(start, depth)], sem_w.at[at]
            )
            copies.append((copy.start, copy.wait))
            at += 1
        steps.append(copies)
    for j in range(min(2, pairs)):
        for start, _ in steps[j]:
            start()
    slot = slot_ref[...]
    order = lax.broadcasted_iota(jnp.int32, (out_ref.shape[0], slot.shape[1]), 0)
    pick = (slot == order).astype(jnp.bfloat16)
    for j in range(pairs):
        for _, wait in steps[j]:
            wait()
        if j + 2 < pairs:
            for start, _ in steps[j + 2]:
                start()
        part = jnp.dot(a_v[j], w_v[j], preferred_element_type=jnp.float32)
        if j == 0:
            acc[...] = part
        else:
            acc[...] += part
    qkv = acc[...].astype(jnp.bfloat16)
    out_ref[...] = jnp.dot(pick, qkv, preferred_element_type=jnp.float32).astype(jnp.bfloat16)


def project(place, slot, own, rows_a, rows_b, chunks, cap, group, groups):
    n_seq, n_fsdp = len(rows_a) + 1, 2 * len(chunks)
    layout = [(mask, change, [flip for flip, _ in parts]) for mask, change, parts in chunks]
    pieces = [part for _, _, parts in chunks for _, part in parts]
    tok, width = own.shape
    depth, cols = width // n_fsdp, pieces[0].shape[1] // groups
    length = n_seq * tok
    pairs = n_fsdp // 2
    return pl.pallas_call(
        functools.partial(project_kernel, n_seq, layout, cap, group),
        out_shape=jax.ShapeDtypeStruct((n_fsdp * cap, cols), jnp.bfloat16),
        in_specs=[SMEM, VMEM] + [ANY] * (2 * n_seq - 1 + len(pieces)),
        out_specs=VMEM,
        scratch_shapes=[
            pltpu.VMEM((pairs, length, 2 * depth), jnp.bfloat16),
            pltpu.VMEM((pairs, 2 * depth, cols), jnp.bfloat16),
            pltpu.VMEM((length, cols), jnp.float32),
            pltpu.SemaphoreType.DMA((pairs, n_seq)),
            pltpu.SemaphoreType.DMA((len(pieces),)),
        ],
        compiler_params=pltpu.CompilerParams(vmem_limit_bytes=VMEM_LIMIT),
        cost_estimate=pl.CostEstimate(
            flops=2 * length * width * cols + 2 * n_fsdp * cap * length * cols,
            bytes_accessed=2 * (length * width + width * cols + n_fsdp * cap * cols),
            transcendentals=0,
        ),
        name="project",
    )(place, slot, own, *rows_a, *rows_b, *pieces)


def attend_kernel(heads, block, place_ref, seg_row, seg_col, cot_ref, in_ref, *refs):
    out_ref, grad_ref, qkv, bias, dk_sum, dv_sum = refs
    size = HEAD_DIMENSION
    length = qkv.shape[0]
    scale = 1.0 / math.sqrt(size)
    key_pos = lax.broadcasted_iota(jnp.int32, (length, length), 0)
    query_pos = lax.broadcasted_iota(jnp.int32, (length, length), 1)
    allowed = (seg_col[...] == seg_row[...]) & (key_pos <= query_pos)
    bias[...] = jnp.where(allowed, 0.0, -1e30)
    spots = lax.broadcasted_iota(jnp.int32, (length, in_ref.shape[0]), 0)
    pick = (spots == place_ref[...]).astype(jnp.bfloat16)
    qkv[...] = jnp.dot(pick, in_ref[...], preferred_element_type=jnp.float32).astype(jnp.bfloat16)
    keys = qkv[:, heads * size : (heads + 1) * size]
    values = qkv[:, (heads + 1) * size : (heads + 2) * size]
    keys_t = keys.T
    values_t = values.T
    dk_sum[...] = jnp.zeros_like(dk_sum)
    dv_sum[...] = jnp.zeros_like(dv_sum)
    for h in range(heads):
        q_h = qkv[:, h * size : (h + 1) * size]
        d_h = cot_ref[:, h * size : (h + 1) * size]
        q_t = q_h.T
        d_t = d_h.T
        for start in range(0, length, block):
            stop = start + block
            scores = jnp.dot(keys[:stop], q_t[:, start:stop], preferred_element_type=jnp.float32)
            scores = scores + bias[:stop, start:stop]
            top = jnp.max(scores, axis=0, keepdims=True)
            weights = jnp.exp2((scores - top) * (scale * math.log2(math.e)))
            probs = weights * (1.0 / jnp.sum(weights, axis=0, keepdims=True))
            probs_b = probs.astype(jnp.bfloat16)
            out_t = jnp.dot(values_t[:, :stop], probs_b, preferred_element_type=jnp.float32).astype(
                jnp.bfloat16
            )
            delta = jnp.sum(
                d_t[:, start:stop].astype(jnp.float32) * out_t.astype(jnp.float32), axis=0, keepdims=True
            )
            dprob = jnp.dot(values[:stop], d_t[:, start:stop], preferred_element_type=jnp.float32)
            dscore = (probs * (dprob - delta)).astype(jnp.bfloat16)
            dq_t = (
                jnp.dot(keys_t[:, :stop], dscore, preferred_element_type=jnp.float32) * scale
            ).astype(jnp.bfloat16)
            dk_sum[:stop] += jnp.dot(dscore, q_h[start:stop], preferred_element_type=jnp.float32)
            dv_sum[:stop] += jnp.dot(probs_b, d_h[start:stop], preferred_element_type=jnp.float32)
            out_ref[start:stop, h * size : (h + 1) * size] = out_t.T
            grad_ref[start:stop, h * size : (h + 1) * size] = dq_t.T
    grad_ref[:, heads * size : (heads + 1) * size] = (dk_sum[...] * scale).astype(jnp.bfloat16)
    grad_ref[:, (heads + 1) * size : (heads + 2) * size] = dv_sum[...].astype(jnp.bfloat16)


def attend(place, segments, cotangent, group, arrived):
    slots, cols = arrived.shape
    size = HEAD_DIMENSION
    heads = cols // size - 2
    length = cotangent.shape[0]
    return pl.pallas_call(
        functools.partial(attend_kernel, heads, 256),
        grid=(1,),
        out_shape=[
            jax.ShapeDtypeStruct((length, heads * size), jnp.bfloat16),
            jax.ShapeDtypeStruct((length, cols), jnp.bfloat16),
        ],
        in_specs=[VMEM, VMEM, VMEM, pl.BlockSpec((length, heads * size), lambda i: (0, group)), VMEM],
        out_specs=[VMEM, VMEM],
        scratch_shapes=[
            pltpu.VMEM((length, cols), jnp.bfloat16),
            pltpu.VMEM((length, length), jnp.float32),
            pltpu.VMEM((length, size), jnp.float32),
            pltpu.VMEM((length, size), jnp.float32),
        ],
        compiler_params=pltpu.CompilerParams(vmem_limit_bytes=VMEM_LIMIT),
        cost_estimate=pl.CostEstimate(
            flops=12 * heads * length * length * size + 2 * length * slots * cols,
            bytes_accessed=2 * (slots * cols + 3 * length * cols),
            transcendentals=heads * length * length,
        ),
        name="attend",
    )(place, segments[None, :], segments[:, None], cotangent, arrived)


def pack_kernel(n_seq, me_ref, slot_ref, spot_ref, *refs):
    own = refs[0]
    rows_a = refs[1:n_seq]
    rows_b = refs[n_seq : 2 * n_seq - 1]
    out_ref, rows_v, slots_v, sem = refs[2 * n_seq - 1 :]
    packs, _, total = slots_v.shape
    sets = slot_ref.shape[0] // n_seq
    span = slot_ref.shape[1]
    each = total // (n_seq * sets)
    odd, z = me_ref[0] & 1, me_ref[1]
    p = pl.program_id(0)
    across = (((1,), (1,)), ((), ()))

    @pl.when(p == 0)
    def _():
        copies = [
            line_copy(own, rows_a, rows_b, k, z, odd, lambda r: r, rows_v.at[k], sem.at[k])
            for k in range(n_seq)
        ]
        for start, _ in copies:
            start()
        order = lax.broadcasted_iota(jnp.int32, (packs * each, span), 0)
        for k in range(n_seq):
            copies[k][1]()
            for g in range(sets):
                at = k * sets + g
                pick = (order == slot_ref[at : at + 1, :]).astype(jnp.bfloat16)
                moved = lax.dot_general(
                    rows_v[k, :, g * span : (g + 1) * span],
                    pick,
                    across,
                    preferred_element_type=jnp.float32,
                ).astype(jnp.bfloat16)
                for q in range(packs):
                    slots_v[q, :, at * each : (at + 1) * each] = moved[:, q * each : (q + 1) * each]

    spots = lax.broadcasted_iota(jnp.int32, (out_ref.shape[1], total), 0)
    pick = (spots == spot_ref[pl.ds(p, 1), :]).astype(jnp.bfloat16)
    out_ref[...] = lax.dot_general(
        slots_v[p], pick, across, preferred_element_type=jnp.float32
    ).astype(jnp.bfloat16)


def pack_columns(place, slot, spot, own, rows_a, rows_b):
    packs, total = spot.shape
    cols, count = own.shape
    n_seq = len(rows_a) + 1
    tokens = n_seq * count
    length = tokens // packs
    return pl.pallas_call(
        functools.partial(pack_kernel, n_seq),
        grid=(packs,),
        out_shape=jax.ShapeDtypeStruct((cols, tokens), jnp.bfloat16),
        in_specs=[
            SMEM,
            pl.BlockSpec(slot.shape, lambda i: (0, 0)),
            pl.BlockSpec(spot.shape, lambda i: (0, 0)),
        ]
        + [ANY] * (2 * n_seq - 1),
        out_specs=pl.BlockSpec((cols, length), lambda i: (0, i)),
        scratch_shapes=[
            pltpu.VMEM((n_seq, cols, count), jnp.bfloat16),
            pltpu.VMEM((packs, cols, total), jnp.bfloat16),
            pltpu.SemaphoreType.DMA((n_seq,)),
        ],
        compiler_params=pltpu.CompilerParams(vmem_limit_bytes=VMEM_LIMIT),
        cost_estimate=pl.CostEstimate(
            flops=4 * packs * total * length * cols,
            bytes_accessed=4 * tokens * cols,
            transcendentals=0,
        ),
        name="pack_columns",
    )(place, slot, spot, own, *rows_a, *rows_b)


def grads_kernel(layout, group, adds, has_before, me_ref, packed_ref, *refs):
    count = sum(len(flips) for _, _, flips in layout)
    before = refs[count : count + 3]
    gq_ref, gk_ref, gv_ref, packed_v, d_v, acc, sem, sem_p, sem_o = refs[
        count + (3 if has_before else 0) :
    ]
    me = me_ref[0]
    steps, width, both = packed_v.shape
    length = both // 2
    cols = d_v.shape[2]
    size = HEAD_DIMENSION
    q_cols = cols - 2 * size

    def results(refs):
        return (
            (acc.at[:, pl.ds(0, q_cols)], refs[0].at[:, pl.ds(group * q_cols, q_cols)]),
            (acc.at[:, pl.ds(q_cols, size)], refs[1].at[:, pl.ds(group * size, size)]),
            (acc.at[:, pl.ds(q_cols + size, size)], refs[2].at[:, pl.ds(group * size, size)]),
        )

    copies = [[] for _ in range(steps)]
    at = 0
    for j, (mask, change, flips) in enumerate(layout):
        for flip in flips:
            start = pl.multiple_of(((me & 1) ^ flip) * length, length)
            copies[j].append(
                pltpu.make_async_copy(refs[at], d_v.at[j, pl.ds(start, length)], sem.at[at])
            )
            at += 1
        start = pl.multiple_of(((me >> 1) ^ (mask + change * (me & 1))) * both, both)
        copies[j].append(
            pltpu.make_async_copy(packed_ref.at[:, pl.ds(start, both)], packed_v.at[j], sem_p.at[j])
        )
    for j in range(min(2, steps)):
        for copy in copies[j]:
            copy.start()
    if adds:
        old = [pltpu.make_async_copy(r, a, sem_o.at[i]) for i, (a, r) in enumerate(results(before))]
        for copy in old:
            copy.start()
        for copy in old:
            copy.wait()
    for j in range(steps):
        for copy in copies[j]:
            copy.wait()
        if j + 2 < steps:
            for copy in copies[j + 2]:
                copy.start()
        part = jnp.dot(packed_v[j], d_v[j], preferred_element_type=jnp.float32)
        if j == 0 and not adds:
            acc[...] = part
        else:
            acc[...] += part
    outs = [
        pltpu.make_async_copy(a, r, sem_o.at[i])
        for i, (a, r) in enumerate(results((gq_ref, gk_ref, gv_ref)))
    ]
    for copy in outs:
        copy.start()
    for copy in outs:
        copy.wait()


def gradients(place, packed, chunks, group, groups, before, adds):
    layout = [(mask, change, [flip for flip, _ in parts]) for mask, change, parts in chunks]
    pieces = [part for _, _, parts in chunks for _, part in parts]
    width = packed.shape[0]
    length, cols = pieces[0].shape
    steps = len(chunks)
    size = HEAD_DIMENSION
    shapes = [
        jax.ShapeDtypeStruct((width, groups * (cols - 2 * size)), jnp.float32),
        jax.ShapeDtypeStruct((width, groups * size), jnp.float32),
        jax.ShapeDtypeStruct((width, groups * size), jnp.float32),
    ]
    extra = [] if before is None else list(before)
    return pl.pallas_call(
        functools.partial(grads_kernel, layout, group, adds, before is not None),
        out_shape=shapes,
        in_specs=[SMEM] + [ANY] * (1 + len(pieces) + len(extra)),
        out_specs=[ANY] * 3,
        input_output_aliases={2 + len(pieces) + i: i for i in range(len(extra))},
        scratch_shapes=[
            pltpu.VMEM((steps, width, 2 * length), jnp.bfloat16),
            pltpu.VMEM((steps, 2 * length, cols), jnp.bfloat16),
            pltpu.VMEM((width, cols), jnp.float32),
            pltpu.SemaphoreType.DMA((len(pieces),)),
            pltpu.SemaphoreType.DMA((steps,)),
            pltpu.SemaphoreType.DMA((3,)),
        ],
        compiler_params=pltpu.CompilerParams(vmem_limit_bytes=VMEM_LIMIT),
        cost_estimate=pl.CostEstimate(
            flops=4 * steps * length * width * cols,
            bytes_accessed=4 * steps * length * (width + cols) + 4 * width * cols,
            transcendentals=0,
        ),
        name="gradients",
    )(place, packed, *pieces, *extra)


def on_device(hidden, destination, segment_ids, cotangent, w_query, key_weight, value_weight):
    tok_rows, width = hidden.shape
    n_fsdp = lax.axis_size("fsdp")
    n_seq = lax.axis_size("seq")
    length = n_seq * tok_rows
    size = HEAD_DIMENSION
    groups = key_weight.shape[1] // size
    q_cols = w_query.shape[1] // groups
    cap = n_seq * n_seq * (2 * tok_rows // (n_fsdp * n_seq))
    f = lax.axis_index("fsdp")
    z = lax.axis_index("seq")
    here = jnp.stack([f, z]).astype(jnp.int32)

    block = jnp.concatenate(
        [
            part[:, g * part.shape[1] // groups : (g + 1) * part.shape[1] // groups]
            for g in range(groups)
            for part in (w_query, key_weight, value_weight)
        ],
        axis=1,
    )
    high = axis_bits(n_fsdp)
    rounds = len(high) == 2 and n_seq == 4 and groups == 2
    gather = gather_all_rounds if rounds else gather_all
    columns = jnp.swapaxes(hidden.reshape(tok_rows, n_fsdp, width // n_fsdp), 0, 1)
    weights, rows_a, rows_b, dest, columns = gather(block, hidden, destination, columns)
    columns = columns.reshape(n_fsdp * tok_rows, -1).T
    mine = lax.dynamic_index_in_dim(dest, f, 0, keepdims=False)

    each = n_seq * (2 * tok_rows // (n_fsdp * n_seq))
    order = jnp.arange(tok_rows, dtype=jnp.int32)
    earlier = order[:, None] < order[None, :]

    def ranks(target):
        same = target[..., :, None] == target[..., None, :]
        return jnp.sum((same & earlier).astype(jnp.int32), axis=-2)

    def from_here(x, axis):
        return lax.dynamic_slice_in_dim(jnp.concatenate([x, x], axis), z, n_seq, axis)

    target = mine // length
    slot = target * cap + jnp.arange(n_seq, dtype=jnp.int32)[:, None] * each + ranks(target)
    slot = from_here(slot, 0).reshape(1, length)
    target = dest // length
    slots = target * each + ranks(target)
    numbers = jnp.arange(n_fsdp * each, dtype=jnp.int32)
    hit = slots[:, :, None, :] == numbers[None, None, :, None]
    spots = jnp.sum(jnp.where(hit, (dest % length + 1)[:, :, None, :], 0), axis=-1) - 1
    span = 128 // each
    within = (jnp.arange(n_fsdp, dtype=jnp.int32) % span)[:, None, None]
    slots = target * (span * each - each) + within * each + slots
    spots = spots.reshape(n_fsdp, n_seq, n_fsdp, each)
    place = lax.dynamic_index_in_dim(spots, f, 2, keepdims=False).reshape(1, n_fsdp * cap)
    slots = jnp.swapaxes(from_here(slots, 1), 0, 1).reshape(-1, span * tok_rows)
    spots = jnp.transpose(from_here(spots, 1), (2, 1, 0, 3)).reshape(n_fsdp, -1)

    def grads_of(packed, parts, group, before, adds=False):
        return gradients(here, packed, parts, group, groups, before, adds)

    exchange = lambda x: lax.all_to_all(x, "fsdp", split_axis=0, concat_axis=0, tiled=True)
    if not rounds:
        sent = [
            project(here, slot, hidden, rows_a, rows_b, weights, cap, g, groups)
            for g in range(groups)
        ]
        results = [
            attend(place, segment_ids[0], cotangent, g, exchange(sent[g])) for g in range(groups)
        ]
        packed = pack_columns(here, slots, spots, columns, *line_gather(columns))
        grads = None
        for g in range(groups):
            grads = grads_of(packed, in_masks(spread(results[g][1], high + [1])), g, grads)
        outs = [out for out, _ in results]
        return (jnp.concatenate(outs, axis=1) if groups > 1 else outs[0], *grads)

    x, y = high
    a1, b1 = line_step(columns, columns)
    sent0 = project(here, slot, hidden, rows_a, rows_b, weights, cap, 0, 2)
    arrived0 = exchange(sent0)
    ((slot, a1, b1, _),) = together((slot, a1, b1, sent0))
    sent1 = project(here, slot, hidden, rows_a, rows_b, weights, cap, 1, 2)
    arrived1 = exchange(sent1)
    a2, b2 = line_step(a1, b1)
    out0, g0 = attend(place, segment_ids[0], cotangent, 0, after(arrived0, sent1))
    ((g0, a2, b2),) = together((g0, a2, b2))
    s0, n0 = swap(g0, "fsdp", 1), by_core(g0, x, y)
    a3, b3 = line_step(a2, b2)
    out1, g1 = attend(place, segment_ids[0], cotangent, 1, after(arrived1, g0))
    ((s0, n0, g1),) = together((s0, n0, g1))
    m0, n1, d0 = by_core(s0, x, y), by_core(g1, x, y), by_core(n0, y, x)
    s1 = swap(g1, "fsdp", 1)
    packed = pack_columns(here, slots, spots, columns, [a1, a2, a3], [b1, b2, b3])
    ((packed, m0, n0, n1, d0, s1),) = together((packed, m0, n0, n1, d0, s1))
    m1, d1 = by_core(s1, x, y), by_core(n1, y, x)
    f0 = [swap(n0, "fsdp", 1), swap(m0, "fsdp", 1)]
    e0 = swap(d0, "fsdp", 1)
    grads = grads_of(packed, in_pairs([g0, s0], [n0, m0], f0, [d0, e0]), 0, None)
    ((m1, d1, n1, *grads),) = together((m1, d1, n1, *grads))
    f1 = [swap(n1, "fsdp", 1), swap(m1, "fsdp", 1)]
    e1 = swap(d1, "fsdp", 1)
    parts = in_pairs([g1, s1], [n1, m1], f1, [d1, e1])
    grads = grads_of(packed, parts[:2], 1, grads)
    grads = grads_of(packed, parts[2:], 1, grads, True)
    return (jnp.concatenate([out0, out1], axis=1), *grads)


def solution(mesh):
    placed = (
        P(("fsdp", "seq"), None),
        P(("fsdp", "seq")),
        P("fsdp", None),
        P("fsdp", "seq"),
        P("fsdp", "seq"),
        P("fsdp", "seq"),
        P("fsdp", "seq"),
    )
    return jax.shard_map(
        on_device,
        mesh=mesh,
        in_specs=placed,
        out_specs=(P("fsdp", "seq"), P("fsdp", "seq"), P("fsdp", "seq"), P("fsdp", "seq")),
        check_vma=False,
    )
```

```python
import functools
import math

import jax
import jax.numpy as jnp
from jax import lax
from jax.experimental import pallas as pl
from jax.experimental.pallas import tpu as pltpu
from jax.sharding import PartitionSpec as P

HEAD_DIMENSION = 128
VMEM_LIMIT = 56 * 1024 * 1024
ANY = pl.BlockSpec(memory_space=pl.ANY)
SMEM = pl.BlockSpec(memory_space=pltpu.SMEM)
VMEM = pl.BlockSpec(memory_space=pltpu.VMEM)


def swap(x, axis, bit):
    n = lax.axis_size(axis)
    return lax.ppermute(x, axis, [(i, i ^ bit) for i in range(n)])


def after(x, *others):
    return lax.optimization_barrier((x, *others))[0] if others else x


def together(*groups):
    flat = lax.optimization_barrier(tuple(x for group in groups for x in group))
    out, at = [], 0
    for group in groups:
        out.append(list(flat[at : at + len(group)]))
        at += len(group)
    return out


def spread(chunk, bits):
    have = {0: chunk}
    for bit in bits:
        for m in sorted(have):
            have[m ^ bit] = swap(have[m], "fsdp", bit)
    return [have[m] for m in range(len(have))]


def axis_bits(n):
    return [1 << i for i in range(1, n.bit_length() - 1)]


def line_step(a, b):
    n_fsdp, n = lax.axis_size("fsdp"), lax.axis_size("seq")

    def pairs(up):
        out = []
        for i in range(n_fsdp):
            for z in range(n):
                to = z + (1 if (i & 1) == up else -1)
                out.append((i * n + z, i * n + to if 0 <= to < n else (i ^ 1) * n + z))
        return out

    return lax.ppermute(a, ("fsdp", "seq"), pairs(0)), lax.ppermute(b, ("fsdp", "seq"), pairs(1))


def line_gather(x):
    a, b = [x], [x]
    for _ in range(1, lax.axis_size("seq")):
        a_next, b_next = line_step(a[-1], b[-1])
        a.append(a_next)
        b.append(b_next)
    return a[1:], b[1:]


def everywhere(x):
    n_fsdp, n_seq = lax.axis_size("fsdp"), lax.axis_size("seq")
    sent = jnp.broadcast_to(x, (n_fsdp * n_seq, *x.shape))
    got = lax.all_to_all(sent, ("fsdp", "seq"), split_axis=0, concat_axis=0, tiled=True)
    return got.reshape(n_fsdp, n_seq, *x.shape)


def by_core(x, even, odd):
    n = lax.axis_size("fsdp")
    return lax.ppermute(x, "fsdp", [(i, i ^ (odd if i & 1 else even)) for i in range(n)])


def in_masks(have):
    return [(j, 0, [(0, have[2 * j]), (1, have[2 * j + 1])]) for j in range(len(have) // 2)]


def in_pairs(own, near, far, diagonal):
    return [
        (0, 0, [(0, own[0]), (1, own[1])]),
        (1, 1, [(0, near[0]), (1, near[1])]),
        (2, -1, [(1, far[0]), (0, far[1])]),
        (3, 0, [(0, diagonal[0]), (1, diagonal[1])]),
    ]


def exchange_columns(blocks):
    return lax.all_to_all(blocks, "fsdp", split_axis=0, concat_axis=0, tiled=True)


def gather_all(block, rows, short, columns, index_of):
    high = axis_bits(lax.axis_size("fsdp"))
    weights = in_masks(spread(block, high + [1]))
    rows_a, rows_b = line_gather(rows)
    short = everywhere(short)
    return weights, rows_a, rows_b, index_of(short), exchange_columns(columns)


def gather_all_rounds(block, rows, short, columns, index_of):
    x, y = axis_bits(lax.axis_size("fsdp"))
    a1, b1 = line_step(rows, rows)
    near = [by_core(block, x, y)]
    sibling = swap(block, "fsdp", 1)
    half = columns.shape[1] // 2
    first, second = exchange_columns(columns[:, :half]), columns[:, half:]
    ((a1, b1, *near, sibling, first, second),) = together((a1, b1, *near, sibling, first, second))
    near.append(by_core(sibling, x, y))
    second = exchange_columns(second)
    a2, b2 = line_step(a1, b1)
    ((a2, b2, *near, short, second),) = together((a2, b2, *near, short, second))
    diagonal = by_core(near[0], y, x)
    a3, b3 = line_step(a2, b2)
    far = [swap(part, "fsdp", 1) for part in near]
    columns = jnp.concatenate([first, second], axis=1)
    index = index_of(everywhere(short))
    (a3, b3, diagonal, columns), far, index = together((a3, b3, diagonal, columns), far, index)
    weights = in_pairs([block, sibling], near, far, [diagonal, swap(diagonal, "fsdp", 1)])
    return weights, [a1, a2, a3], [b1, b2, b3], index, columns


def line_copy(own, a, b, k, z, odd, view, spot, sem):
    if k == 0:
        copy = pltpu.make_async_copy(view(own), spot, sem)
        return copy.start, copy.wait
    n = len(a) + 1
    above = [pltpu.make_async_copy(view(r[k - 1]), spot, sem) for r in (b, a)]
    below = [pltpu.make_async_copy(view(r[n - k - 1]), spot, sem) for r in (a, b)]

    def start():
        for i in range(2):
            pl.when((z + k < n) & (odd == i))(above[i].start)
            pl.when((z + k >= n) & (odd == i))(below[i].start)

    return start, above[0].wait


def project_kernel(n_seq, layout, cap, group, me_ref, slot_ref, *refs):
    own = refs[0]
    rows_a = refs[1:n_seq]
    rows_b = refs[n_seq : 2 * n_seq - 1]
    count = sum(len(flips) for _, _, flips in layout)
    chunks = refs[2 * n_seq - 1 : 2 * n_seq - 1 + count]
    out_ref, a_v, w_v, acc, sem_a, sem_w = refs[2 * n_seq - 1 + count :]
    me, z = me_ref[0], me_ref[1]
    tok = own.shape[0]
    pairs, both, cols = w_v.shape
    depth = both // 2
    steps = []
    at = 0
    for j, (mask, change, flips) in enumerate(layout):
        pair = (me >> 1) ^ (mask + change * (me & 1))
        columns = pl.ds(pl.multiple_of(pair * both, both), both)
        copies = []
        for k in range(n_seq):
            spot = a_v.at[j, pl.ds(k * tok, tok)]
            copies.append(
                line_copy(own, rows_a, rows_b, k, z, me & 1, lambda r, c=columns: r.at[:, c], spot, sem_a.at[j, k])
            )
        for flip in flips:
            start = pl.multiple_of(((me & 1) ^ flip) * depth, depth)
            copy = pltpu.make_async_copy(
                chunks[at].at[:, pl.ds(group * cols, cols)], w_v.at[j, pl.ds(start, depth)], sem_w.at[at]
            )
            copies.append((copy.start, copy.wait))
            at += 1
        steps.append(copies)
    for j in range(min(2, pairs)):
        for start, _ in steps[j]:
            start()
    slot = slot_ref[...]
    order = lax.broadcasted_iota(jnp.int32, (out_ref.shape[0], slot.shape[1]), 0)
    pick = (slot == order).astype(jnp.bfloat16)
    for j in range(pairs):
        for _, wait in steps[j]:
            wait()
        if j + 2 < pairs:
            for start, _ in steps[j + 2]:
                start()
        part = jnp.dot(a_v[j], w_v[j], preferred_element_type=jnp.float32)
        if j == 0:
            acc[...] = part
        else:
            acc[...] += part
    qkv = acc[...].astype(jnp.bfloat16)
    out_ref[...] = jnp.dot(pick, qkv, preferred_element_type=jnp.float32).astype(jnp.bfloat16)


def project(place, slot, own, rows_a, rows_b, chunks, cap, group, groups):
    n_seq, n_fsdp = len(rows_a) + 1, 2 * len(chunks)
    layout = [(mask, change, [flip for flip, _ in parts]) for mask, change, parts in chunks]
    pieces = [part for _, _, parts in chunks for _, part in parts]
    tok, width = own.shape
    depth, cols = width // n_fsdp, pieces[0].shape[1] // groups
    length = n_seq * tok
    pairs = n_fsdp // 2
    return pl.pallas_call(
        functools.partial(project_kernel, n_seq, layout, cap, group),
        out_shape=jax.ShapeDtypeStruct((n_fsdp * cap, cols), jnp.bfloat16),
        in_specs=[SMEM, VMEM] + [ANY] * (2 * n_seq - 1 + len(pieces)),
        out_specs=VMEM,
        scratch_shapes=[
            pltpu.VMEM((pairs, length, 2 * depth), jnp.bfloat16),
            pltpu.VMEM((pairs, 2 * depth, cols), jnp.bfloat16),
            pltpu.VMEM((length, cols), jnp.float32),
            pltpu.SemaphoreType.DMA((pairs, n_seq)),
            pltpu.SemaphoreType.DMA((len(pieces),)),
        ],
        compiler_params=pltpu.CompilerParams(vmem_limit_bytes=VMEM_LIMIT),
        cost_estimate=pl.CostEstimate(
            flops=2 * length * width * cols + 2 * n_fsdp * cap * length * cols,
            bytes_accessed=2 * (length * width + width * cols + n_fsdp * cap * cols),
            transcendentals=0,
        ),
        name="project",
    )(place, slot, own, *rows_a, *rows_b, *pieces)


def attend_kernel(heads, block, abreast, place_ref, seg_row, seg_col, cot_ref, in_ref, *refs):
    out_ref, grad_ref, qkv, bias, dk_sum, dv_sum = refs
    size = HEAD_DIMENSION
    length = qkv.shape[0]
    scale = 1.0 / math.sqrt(size)
    key_pos = lax.broadcasted_iota(jnp.int32, (length, length), 0)
    query_pos = lax.broadcasted_iota(jnp.int32, (length, length), 1)
    allowed = (seg_col[...] == seg_row[...]) & (key_pos <= query_pos)
    bias[...] = jnp.where(allowed, 0.0, -1e30)
    spots = lax.broadcasted_iota(jnp.int32, (length, in_ref.shape[0]), 0)
    pick = (spots == place_ref[...]).astype(jnp.bfloat16)
    qkv[...] = jnp.dot(pick, in_ref[...], preferred_element_type=jnp.float32).astype(jnp.bfloat16)
    keys = qkv[:, heads * size : (heads + 1) * size]
    values = qkv[:, (heads + 1) * size : (heads + 2) * size]
    keys_t = keys.T
    values_t = values.T
    dk_sum[...] = jnp.zeros_like(dk_sum)
    dv_sum[...] = jnp.zeros_like(dv_sum)
    starts = list(range(0, length, block))
    for first in range(0, heads, abreast):
        items = [
            (h, start, start + block)
            for h in range(first, min(first + abreast, heads))
            for start in starts
        ]
        q_t = {h: qkv[:, h * size : (h + 1) * size].T for h, _, _ in items}
        d_t = {h: cot_ref[:, h * size : (h + 1) * size].T for h, _, _ in items}
        scores = [
            jnp.dot(keys[:stop], q_t[h][:, start:stop], preferred_element_type=jnp.float32)
            + bias[:stop, start:stop]
            for h, start, stop in items
        ]
        dprob = [
            jnp.dot(values[:stop], d_t[h][:, start:stop], preferred_element_type=jnp.float32)
            for h, start, stop in items
        ]
        top = [jnp.max(x, axis=0, keepdims=True) for x in scores]
        weights = [
            jnp.exp2((x - t) * (scale * math.log2(math.e))) for x, t in zip(scores, top)
        ]
        probs = [x * (1.0 / jnp.sum(x, axis=0, keepdims=True)) for x in weights]
        probs_b = [x.astype(jnp.bfloat16) for x in probs]
        out_t = [
            jnp.dot(values_t[:, :stop], x, preferred_element_type=jnp.float32).astype(jnp.bfloat16)
            for (_, _, stop), x in zip(items, probs_b)
        ]
        delta = [
            jnp.sum(
                d_t[h][:, start:stop].astype(jnp.float32) * x.astype(jnp.float32),
                axis=0,
                keepdims=True,
            )
            for (h, start, stop), x in zip(items, out_t)
        ]
        dscore = [
            (p * (x - t)).astype(jnp.bfloat16) for p, x, t in zip(probs, dprob, delta)
        ]
        dq_t = [
            (jnp.dot(keys_t[:, :stop], x, preferred_element_type=jnp.float32) * scale).astype(
                jnp.bfloat16
            )
            for (_, _, stop), x in zip(items, dscore)
        ]
        for (h, start, stop), x, p, o, q in zip(items, dscore, probs_b, out_t, dq_t):
            columns = slice(h * size, (h + 1) * size)
            dk_sum[:stop] += jnp.dot(x, qkv[start:stop, columns], preferred_element_type=jnp.float32)
            dv_sum[:stop] += jnp.dot(p, cot_ref[start:stop, columns], preferred_element_type=jnp.float32)
            out_ref[start:stop, columns] = o.T
            grad_ref[start:stop, columns] = q.T
    grad_ref[:, heads * size : (heads + 1) * size] = (dk_sum[...] * scale).astype(jnp.bfloat16)
    grad_ref[:, (heads + 1) * size : (heads + 2) * size] = dv_sum[...].astype(jnp.bfloat16)


def attend(place, segments, cotangent, group, arrived):
    slots, cols = arrived.shape
    size = HEAD_DIMENSION
    heads = cols // size - 2
    length = cotangent.shape[0]
    abreast = max(1, 5 * 512 * 512 // (length * length))
    return pl.pallas_call(
        functools.partial(attend_kernel, heads, 256, abreast),
        grid=(1,),
        out_shape=[
            jax.ShapeDtypeStruct((length, heads * size), jnp.bfloat16),
            jax.ShapeDtypeStruct((length, cols), jnp.bfloat16),
        ],
        in_specs=[VMEM, VMEM, VMEM, pl.BlockSpec((length, heads * size), lambda i: (0, group)), VMEM],
        out_specs=[VMEM, VMEM],
        scratch_shapes=[
            pltpu.VMEM((length, cols), jnp.bfloat16),
            pltpu.VMEM((length, length), jnp.float32),
            pltpu.VMEM((length, size), jnp.float32),
            pltpu.VMEM((length, size), jnp.float32),
        ],
        compiler_params=pltpu.CompilerParams(vmem_limit_bytes=VMEM_LIMIT),
        cost_estimate=pl.CostEstimate(
            flops=12 * heads * length * length * size + 2 * length * slots * cols,
            bytes_accessed=2 * (slots * cols + 3 * length * cols),
            transcendentals=heads * length * length,
        ),
        name="attend",
    )(place, segments[None, :], segments[:, None], cotangent, arrived)


def pack_kernel(n_seq, me_ref, slot_ref, spot_ref, *refs):
    own = refs[0]
    rows_a = refs[1:n_seq]
    rows_b = refs[n_seq : 2 * n_seq - 1]
    out_ref, rows_v, slots_v, sem = refs[2 * n_seq - 1 :]
    packs, _, total = slots_v.shape
    sets = slot_ref.shape[0] // n_seq
    span = slot_ref.shape[1]
    each = total // (n_seq * sets)
    odd, z = me_ref[0] & 1, me_ref[1]
    p = pl.program_id(0)
    across = (((1,), (1,)), ((), ()))

    @pl.when(p == 0)
    def _():
        copies = [
            line_copy(own, rows_a, rows_b, k, z, odd, lambda r: r, rows_v.at[k], sem.at[k])
            for k in range(n_seq)
        ]
        for start, _ in copies:
            start()
        order = lax.broadcasted_iota(jnp.int32, (packs * each, span), 0)
        for k in range(n_seq):
            copies[k][1]()
            for g in range(sets):
                at = k * sets + g
                pick = (order == slot_ref[at : at + 1, :]).astype(jnp.bfloat16)
                tok = rows_v.shape[3]
                pieces = [rows_v[k, i] for i in range(g * span // tok, (g + 1) * span // tok)]
                moved = lax.dot_general(
                    jnp.concatenate(pieces, axis=1),
                    pick,
                    across,
                    preferred_element_type=jnp.float32,
                ).astype(jnp.bfloat16)
                for q in range(packs):
                    slots_v[q, :, at * each : (at + 1) * each] = moved[:, q * each : (q + 1) * each]

    spots = lax.broadcasted_iota(jnp.int32, (out_ref.shape[1], total), 0)
    pick = (spots == spot_ref[pl.ds(p, 1), :]).astype(jnp.bfloat16)
    out_ref[...] = lax.dot_general(
        slots_v[p], pick, across, preferred_element_type=jnp.float32
    ).astype(jnp.bfloat16)


def pack_columns(place, slot, spot, own, rows_a, rows_b):
    packs, total = spot.shape
    n_fsdp, cols, tok = own.shape
    n_seq = len(rows_a) + 1
    tokens = n_seq * n_fsdp * tok
    length = tokens // packs
    return pl.pallas_call(
        functools.partial(pack_kernel, n_seq),
        grid=(packs,),
        out_shape=jax.ShapeDtypeStruct((cols, tokens), jnp.bfloat16),
        in_specs=[
            SMEM,
            pl.BlockSpec(slot.shape, lambda i: (0, 0)),
            pl.BlockSpec(spot.shape, lambda i: (0, 0)),
        ]
        + [ANY] * (2 * n_seq - 1),
        out_specs=pl.BlockSpec((cols, length), lambda i: (0, i)),
        scratch_shapes=[
            pltpu.VMEM((n_seq, n_fsdp, cols, tok), jnp.bfloat16),
            pltpu.VMEM((packs, cols, total), jnp.bfloat16),
            pltpu.SemaphoreType.DMA((n_seq,)),
        ],
        compiler_params=pltpu.CompilerParams(vmem_limit_bytes=VMEM_LIMIT),
        cost_estimate=pl.CostEstimate(
            flops=4 * packs * total * length * cols,
            bytes_accessed=4 * tokens * cols,
            transcendentals=0,
        ),
        name="pack_columns",
    )(place, slot, spot, own, *rows_a, *rows_b)


def grads_kernel(layout, group, adds, has_before, me_ref, packed_ref, *refs):
    count = sum(len(flips) for _, _, flips in layout)
    before = refs[count : count + 3]
    gq_ref, gk_ref, gv_ref, packed_v, d_v, acc, sem, sem_p, sem_o = refs[
        count + (3 if has_before else 0) :
    ]
    me = me_ref[0]
    steps, width, both = packed_v.shape
    length = both // 2
    cols = d_v.shape[2]
    size = HEAD_DIMENSION
    q_cols = cols - 2 * size

    def results(refs):
        return (
            (acc.at[:, pl.ds(0, q_cols)], refs[0].at[:, pl.ds(group * q_cols, q_cols)]),
            (acc.at[:, pl.ds(q_cols, size)], refs[1].at[:, pl.ds(group * size, size)]),
            (acc.at[:, pl.ds(q_cols + size, size)], refs[2].at[:, pl.ds(group * size, size)]),
        )

    copies = [[] for _ in range(steps)]
    at = 0
    for j, (mask, change, flips) in enumerate(layout):
        for flip in flips:
            start = pl.multiple_of(((me & 1) ^ flip) * length, length)
            copies[j].append(
                pltpu.make_async_copy(refs[at], d_v.at[j, pl.ds(start, length)], sem.at[at])
            )
            at += 1
        start = pl.multiple_of(((me >> 1) ^ (mask + change * (me & 1))) * both, both)
        copies[j].append(
            pltpu.make_async_copy(packed_ref.at[:, pl.ds(start, both)], packed_v.at[j], sem_p.at[j])
        )
    for j in range(min(2, steps)):
        for copy in copies[j]:
            copy.start()
    if adds:
        old = [pltpu.make_async_copy(r, a, sem_o.at[i]) for i, (a, r) in enumerate(results(before))]
        for copy in old:
            copy.start()
    for j in range(steps):
        for copy in copies[j]:
            copy.wait()
        if j + 2 < steps:
            for copy in copies[j + 2]:
                copy.start()
        part = jnp.dot(packed_v[j], d_v[j], preferred_element_type=jnp.float32)
        if j == 0 and adds:
            for copy in old:
                copy.wait()
        if j == 0 and not adds:
            acc[...] = part
        else:
            acc[...] += part
    outs = [
        pltpu.make_async_copy(a, r, sem_o.at[i])
        for i, (a, r) in enumerate(results((gq_ref, gk_ref, gv_ref)))
    ]
    for copy in outs:
        copy.start()
    for copy in outs:
        copy.wait()


def gradients(place, packed, chunks, group, groups, before, adds):
    layout = [(mask, change, [flip for flip, _ in parts]) for mask, change, parts in chunks]
    pieces = [part for _, _, parts in chunks for _, part in parts]
    width = packed.shape[0]
    length, cols = pieces[0].shape
    steps = len(chunks)
    size = HEAD_DIMENSION
    shapes = [
        jax.ShapeDtypeStruct((width, groups * (cols - 2 * size)), jnp.float32),
        jax.ShapeDtypeStruct((width, groups * size), jnp.float32),
        jax.ShapeDtypeStruct((width, groups * size), jnp.float32),
    ]
    extra = [] if before is None else list(before)
    return pl.pallas_call(
        functools.partial(grads_kernel, layout, group, adds, before is not None),
        out_shape=shapes,
        in_specs=[SMEM] + [ANY] * (1 + len(pieces) + len(extra)),
        out_specs=[ANY] * 3,
        input_output_aliases={2 + len(pieces) + i: i for i in range(len(extra))},
        scratch_shapes=[
            pltpu.VMEM((steps, width, 2 * length), jnp.bfloat16),
            pltpu.VMEM((steps, 2 * length, cols), jnp.bfloat16),
            pltpu.VMEM((width, cols), jnp.float32),
            pltpu.SemaphoreType.DMA((len(pieces),)),
            pltpu.SemaphoreType.DMA((steps,)),
            pltpu.SemaphoreType.DMA((3,)),
        ],
        compiler_params=pltpu.CompilerParams(vmem_limit_bytes=VMEM_LIMIT),
        cost_estimate=pl.CostEstimate(
            flops=4 * steps * length * width * cols,
            bytes_accessed=4 * steps * length * (width + cols) + 4 * width * cols,
            transcendentals=0,
        ),
        name="gradients",
    )(place, packed, *pieces, *extra)


def on_device(hidden, destination, segment_ids, cotangent, w_query, key_weight, value_weight):
    tok_rows, width = hidden.shape
    n_fsdp = lax.axis_size("fsdp")
    n_seq = lax.axis_size("seq")
    length = n_seq * tok_rows
    size = HEAD_DIMENSION
    groups = key_weight.shape[1] // size
    q_cols = w_query.shape[1] // groups
    cap = n_seq * n_seq * (2 * tok_rows // (n_fsdp * n_seq))
    f = lax.axis_index("fsdp")
    z = lax.axis_index("seq")
    here = jnp.stack([f, z]).astype(jnp.int32)

    block = jnp.concatenate(
        [
            part[:, g * part.shape[1] // groups : (g + 1) * part.shape[1] // groups]
            for g in range(groups)
            for part in (w_query, key_weight, value_weight)
        ],
        axis=1,
    )
    high = axis_bits(n_fsdp)
    rounds = len(high) == 2 and n_seq == 4 and groups == 2
    gather = gather_all_rounds if rounds else gather_all
    columns = jnp.transpose(hidden.reshape(tok_rows, n_fsdp, width // n_fsdp), (1, 2, 0))
    each = n_seq * (2 * tok_rows // (n_fsdp * n_seq))
    order = jnp.arange(tok_rows, dtype=jnp.int32)
    earlier = order[:, None] < order[None, :]

    def ranks(target):
        same = target[..., :, None] == target[..., None, :]
        return jnp.sum((same & earlier).astype(jnp.int32), axis=-2)

    def from_here(x, axis):
        return lax.dynamic_slice_in_dim(jnp.concatenate([x, x], axis), z, n_seq, axis)

    def index_of(dest):
        mine = lax.dynamic_index_in_dim(dest, f, 0, keepdims=False)
        target = mine // length
        slot = target * cap + jnp.arange(n_seq, dtype=jnp.int32)[:, None] * each + ranks(target)
        slot = from_here(slot, 0).reshape(1, length)
        target = dest // length
        slots = target * each + ranks(target)
        numbers = jnp.arange(n_fsdp * each, dtype=jnp.int32)
        hit = slots[:, :, None, :] == numbers[None, None, :, None]
        spots = jnp.sum(jnp.where(hit, (dest % length + 1)[:, :, None, :], 0), axis=-1) - 1
        span = 128 // each
        within = (jnp.arange(n_fsdp, dtype=jnp.int32) % span)[:, None, None]
        slots = target * (span * each - each) + within * each + slots
        spots = spots.reshape(n_fsdp, n_seq, n_fsdp, each)
        place = lax.dynamic_index_in_dim(spots, f, 2, keepdims=False).reshape(1, n_fsdp * cap)
        slots = jnp.swapaxes(from_here(slots, 1), 0, 1).reshape(-1, span * tok_rows)
        spots = jnp.transpose(from_here(spots, 1), (2, 1, 0, 3)).reshape(n_fsdp, -1)
        return slot, place, slots, spots

    weights, rows_a, rows_b, index, columns = gather(block, hidden, destination, columns, index_of)
    slot, place, slots, spots = index

    def grads_of(packed, parts, group, before, adds=False):
        return gradients(here, packed, parts, group, groups, before, adds)

    exchange = lambda x: lax.all_to_all(x, "fsdp", split_axis=0, concat_axis=0, tiled=True)
    if not rounds:
        sent = [
            project(here, slot, hidden, rows_a, rows_b, weights, cap, g, groups)
            for g in range(groups)
        ]
        results = [
            attend(place, segment_ids[0], cotangent, g, exchange(sent[g])) for g in range(groups)
        ]
        packed = pack_columns(here, slots, spots, columns, *line_gather(columns))
        grads = None
        for g in range(groups):
            grads = grads_of(packed, in_masks(spread(results[g][1], high + [1])), g, grads)
        outs = [out for out, _ in results]
        return (jnp.concatenate(outs, axis=1) if groups > 1 else outs[0], *grads)

    x, y = high
    a1, b1 = line_step(columns, columns)
    sent0 = project(here, slot, hidden, rows_a, rows_b, weights, cap, 0, 2)
    arrived0 = exchange(sent0)
    ((slot, a1, b1, _),) = together((slot, a1, b1, sent0))
    sent1 = project(here, slot, hidden, rows_a, rows_b, weights, cap, 1, 2)
    arrived1 = exchange(sent1)
    a2, b2 = line_step(a1, b1)
    out0, g0 = attend(place, segment_ids[0], cotangent, 0, after(arrived0, sent1))
    ((g0, a2, b2),) = together((g0, a2, b2))
    s0, n0 = swap(g0, "fsdp", 1), by_core(g0, x, y)
    a3, b3 = line_step(a2, b2)
    out1, g1 = attend(place, segment_ids[0], cotangent, 1, after(arrived1, g0))
    ((s0, n0, g1),) = together((s0, n0, g1))
    m0, n1, d0 = by_core(s0, x, y), by_core(g1, x, y), by_core(n0, y, x)
    s1 = swap(g1, "fsdp", 1)
    packed = pack_columns(here, slots, spots, columns, [a1, a2, a3], [b1, b2, b3])
    ((packed, m0, n0, n1, d0, s1),) = together((packed, m0, n0, n1, d0, s1))
    m1, d1 = by_core(s1, x, y), by_core(n1, y, x)
    f0 = [swap(n0, "fsdp", 1), swap(m0, "fsdp", 1)]
    e0 = swap(d0, "fsdp", 1)
    grads = grads_of(packed, in_pairs([g0, s0], [n0, m0], f0, [d0, e0]), 0, None)
    attn_out = jnp.concatenate([out0, out1], axis=1)
    ((m1, d1, n1, attn_out, *grads),) = together((m1, d1, n1, attn_out, *grads))
    f1 = [swap(n1, "fsdp", 1), swap(m1, "fsdp", 1)]
    e1 = swap(d1, "fsdp", 1)
    parts = in_pairs([g1, s1], [n1, m1], f1, [d1, e1])
    grads = grads_of(packed, parts[:2], 1, grads)
    grads = grads_of(packed, parts[2:], 1, grads, True)
    return (attn_out, *grads)


def solution(mesh):
    placed = (
        P(("fsdp", "seq"), None),
        P(("fsdp", "seq")),
        P("fsdp", None),
        P("fsdp", "seq"),
        P("fsdp", "seq"),
        P("fsdp", "seq"),
        P("fsdp", "seq"),
    )
    return jax.shard_map(
        on_device,
        mesh=mesh,
        in_specs=placed,
        out_specs=(P("fsdp", "seq"), P("fsdp", "seq"), P("fsdp", "seq"), P("fsdp", "seq")),
        check_vma=False,
    )
```

```python
import functools
import math

import jax
import jax.numpy as jnp
from jax import lax
from jax.experimental import pallas as pl
from jax.experimental.pallas import tpu as pltpu
from jax.sharding import PartitionSpec as P

HEAD_DIMENSION = 128
VMEM_LIMIT = 56 * 1024 * 1024
ANY = pl.BlockSpec(memory_space=pl.ANY)
SMEM = pl.BlockSpec(memory_space=pltpu.SMEM)
VMEM = pl.BlockSpec(memory_space=pltpu.VMEM)


def swap(x, axis, bit):
    n = lax.axis_size(axis)
    return lax.ppermute(x, axis, [(i, i ^ bit) for i in range(n)])


def after(x, *others):
    return lax.optimization_barrier((x, *others))[0] if others else x


def together(*groups):
    flat = lax.optimization_barrier(tuple(x for group in groups for x in group))
    out, at = [], 0
    for group in groups:
        out.append(list(flat[at : at + len(group)]))
        at += len(group)
    return out


def spread(chunk, bits):
    have = {0: chunk}
    for bit in bits:
        for m in sorted(have):
            have[m ^ bit] = swap(have[m], "fsdp", bit)
    return [have[m] for m in range(len(have))]


def axis_bits(n):
    return [1 << i for i in range(1, n.bit_length() - 1)]


def line_step(a, b):
    n_fsdp, n = lax.axis_size("fsdp"), lax.axis_size("seq")

    def pairs(up):
        out = []
        for i in range(n_fsdp):
            for z in range(n):
                to = z + (1 if (i & 1) == up else -1)
                out.append((i * n + z, i * n + to if 0 <= to < n else (i ^ 1) * n + z))
        return out

    return lax.ppermute(a, ("fsdp", "seq"), pairs(0)), lax.ppermute(b, ("fsdp", "seq"), pairs(1))


def line_gather(x):
    a, b = [x], [x]
    for _ in range(1, lax.axis_size("seq")):
        a_next, b_next = line_step(a[-1], b[-1])
        a.append(a_next)
        b.append(b_next)
    return a[1:], b[1:]


def everywhere(x):
    n_fsdp, n_seq = lax.axis_size("fsdp"), lax.axis_size("seq")
    sent = jnp.broadcast_to(x, (n_fsdp * n_seq, *x.shape))
    got = lax.all_to_all(sent, ("fsdp", "seq"), split_axis=0, concat_axis=0, tiled=True)
    return got.reshape(n_fsdp, n_seq, *x.shape)


def by_core(x, even, odd):
    n = lax.axis_size("fsdp")
    return lax.ppermute(x, "fsdp", [(i, i ^ (odd if i & 1 else even)) for i in range(n)])


def in_masks(have):
    return [(j, 0, [(0, have[2 * j]), (1, have[2 * j + 1])]) for j in range(len(have) // 2)]


def in_pairs(own, near, far, diagonal):
    return [
        (0, 0, [(0, own[0]), (1, own[1])]),
        (1, 1, [(0, near[0]), (1, near[1])]),
        (2, -1, [(1, far[0]), (0, far[1])]),
        (3, 0, [(0, diagonal[0]), (1, diagonal[1])]),
    ]


def exchange_columns(blocks):
    return lax.all_to_all(blocks, "fsdp", split_axis=0, concat_axis=0, tiled=True)


def gather_all(block, rows, short, columns, index_of):
    high = axis_bits(lax.axis_size("fsdp"))
    weights = in_masks(spread(block, high + [1]))
    rows_a, rows_b = line_gather(rows)
    short = everywhere(short)
    return weights, rows_a, rows_b, index_of(short), exchange_columns(columns)


def gather_all_rounds(block, rows, short, columns, index_of):
    x, y = axis_bits(lax.axis_size("fsdp"))
    a1, b1 = line_step(rows, rows)
    near = [by_core(block, x, y)]
    sibling = swap(block, "fsdp", 1)
    short = everywhere(short)
    ((a1, b1, *near, sibling, columns, short),) = together((a1, b1, *near, sibling, columns, short))
    near.append(by_core(sibling, x, y))
    columns = exchange_columns(columns)
    a2, b2 = line_step(a1, b1)
    index = index_of(short)
    (a2, b2, columns), near, index = together((a2, b2, columns), near, index)
    diagonal = by_core(near[0], y, x)
    a3, b3 = line_step(a2, b2)
    far = [swap(part, "fsdp", 1) for part in near]
    (a3, b3, diagonal, columns), far = together((a3, b3, diagonal, columns), far)
    weights = in_pairs([block, sibling], near, far, [diagonal, swap(diagonal, "fsdp", 1)])
    return weights, [a1, a2, a3], [b1, b2, b3], index, columns


def line_copy(own, a, b, k, z, odd, view, spot, sem):
    if k == 0:
        copy = pltpu.make_async_copy(view(own), spot, sem)
        return copy.start, copy.wait
    n = len(a) + 1
    above = [pltpu.make_async_copy(view(r[k - 1]), spot, sem) for r in (b, a)]
    below = [pltpu.make_async_copy(view(r[n - k - 1]), spot, sem) for r in (a, b)]

    def start():
        for i in range(2):
            pl.when((z + k < n) & (odd == i))(above[i].start)
            pl.when((z + k >= n) & (odd == i))(below[i].start)

    return start, above[0].wait


def project_kernel(n_seq, layout, cap, group, me_ref, slot_ref, *refs):
    own = refs[0]
    rows_a = refs[1:n_seq]
    rows_b = refs[n_seq : 2 * n_seq - 1]
    count = sum(len(flips) for _, _, flips in layout)
    chunks = refs[2 * n_seq - 1 : 2 * n_seq - 1 + count]
    out_ref, a_v, w_v, acc, sem_a, sem_w = refs[2 * n_seq - 1 + count :]
    me, z = me_ref[0], me_ref[1]
    tok = own.shape[0]
    pairs, both, cols = w_v.shape
    depth = both // 2
    steps = []
    at = 0
    for j, (mask, change, flips) in enumerate(layout):
        pair = (me >> 1) ^ (mask + change * (me & 1))
        columns = pl.ds(pl.multiple_of(pair * both, both), both)
        copies = []
        for k in range(n_seq):
            spot = a_v.at[j, pl.ds(k * tok, tok)]
            copies.append(
                line_copy(own, rows_a, rows_b, k, z, me & 1, lambda r, c=columns: r.at[:, c], spot, sem_a.at[j, k])
            )
        for flip in flips:
            start = pl.multiple_of(((me & 1) ^ flip) * depth, depth)
            copy = pltpu.make_async_copy(
                chunks[at].at[:, pl.ds(group * cols, cols)], w_v.at[j, pl.ds(start, depth)], sem_w.at[at]
            )
            copies.append((copy.start, copy.wait))
            at += 1
        steps.append(copies)
    for j in range(min(2, pairs)):
        for start, _ in steps[j]:
            start()
    slot = slot_ref[...]
    order = lax.broadcasted_iota(jnp.int32, (out_ref.shape[0], slot.shape[1]), 0)
    pick = (slot == order).astype(jnp.bfloat16)
    for j in range(pairs):
        for _, wait in steps[j]:
            wait()
        if j + 2 < pairs:
            for start, _ in steps[j + 2]:
                start()
        part = jnp.dot(a_v[j], w_v[j], preferred_element_type=jnp.float32)
        if j == 0:
            acc[...] = part
        else:
            acc[...] += part
    qkv = acc[...].astype(jnp.bfloat16)
    out_ref[...] = jnp.dot(pick, qkv, preferred_element_type=jnp.float32).astype(jnp.bfloat16)


def project(place, slot, own, rows_a, rows_b, chunks, cap, group, groups):
    n_seq, n_fsdp = len(rows_a) + 1, 2 * len(chunks)
    layout = [(mask, change, [flip for flip, _ in parts]) for mask, change, parts in chunks]
    pieces = [part for _, _, parts in chunks for _, part in parts]
    tok, width = own.shape
    depth, cols = width // n_fsdp, pieces[0].shape[1] // groups
    length = n_seq * tok
    pairs = n_fsdp // 2
    return pl.pallas_call(
        functools.partial(project_kernel, n_seq, layout, cap, group),
        out_shape=jax.ShapeDtypeStruct((n_fsdp * cap, cols), jnp.bfloat16),
        in_specs=[SMEM, VMEM] + [ANY] * (2 * n_seq - 1 + len(pieces)),
        out_specs=VMEM,
        scratch_shapes=[
            pltpu.VMEM((pairs, length, 2 * depth), jnp.bfloat16),
            pltpu.VMEM((pairs, 2 * depth, cols), jnp.bfloat16),
            pltpu.VMEM((length, cols), jnp.float32),
            pltpu.SemaphoreType.DMA((pairs, n_seq)),
            pltpu.SemaphoreType.DMA((len(pieces),)),
        ],
        compiler_params=pltpu.CompilerParams(vmem_limit_bytes=VMEM_LIMIT),
        cost_estimate=pl.CostEstimate(
            flops=2 * length * width * cols + 2 * n_fsdp * cap * length * cols,
            bytes_accessed=2 * (length * width + width * cols + n_fsdp * cap * cols),
            transcendentals=0,
        ),
        name="project",
    )(place, slot, own, *rows_a, *rows_b, *pieces)


def attend_kernel(heads, block, abreast, place_ref, seg_row, seg_col, cot_ref, in_ref, *refs):
    out_ref, grad_ref, qkv, bias, dk_sum, dv_sum = refs
    size = HEAD_DIMENSION
    length = qkv.shape[0]
    scale = 1.0 / math.sqrt(size)
    key_pos = lax.broadcasted_iota(jnp.int32, (length, length), 0)
    query_pos = lax.broadcasted_iota(jnp.int32, (length, length), 1)
    allowed = (seg_col[...] == seg_row[...]) & (key_pos <= query_pos)
    bias[...] = jnp.where(allowed, 0.0, -1e30)
    spots = lax.broadcasted_iota(jnp.int32, (length, in_ref.shape[0]), 0)
    pick = (spots == place_ref[...]).astype(jnp.bfloat16)
    qkv[...] = jnp.dot(pick, in_ref[...], preferred_element_type=jnp.float32).astype(jnp.bfloat16)
    keys = qkv[:, heads * size : (heads + 1) * size]
    values = qkv[:, (heads + 1) * size : (heads + 2) * size]
    keys_t = keys.T
    values_t = values.T
    dk_sum[...] = jnp.zeros_like(dk_sum)
    dv_sum[...] = jnp.zeros_like(dv_sum)
    starts = list(range(0, length, block))
    for first in range(0, heads, abreast):
        items = [
            (h, start, start + block)
            for h in range(first, min(first + abreast, heads))
            for start in starts
        ]
        q_t = {h: qkv[:, h * size : (h + 1) * size].T for h, _, _ in items}
        d_t = {h: cot_ref[:, h * size : (h + 1) * size].T for h, _, _ in items}
        scores = [
            jnp.dot(keys[:stop], q_t[h][:, start:stop], preferred_element_type=jnp.float32)
            + bias[:stop, start:stop]
            for h, start, stop in items
        ]
        dprob = [
            jnp.dot(values[:stop], d_t[h][:, start:stop], preferred_element_type=jnp.float32)
            for h, start, stop in items
        ]
        top = [jnp.max(x, axis=0, keepdims=True) for x in scores]
        weights = [
            jnp.exp2((x - t) * (scale * math.log2(math.e))) for x, t in zip(scores, top)
        ]
        probs = [x * (1.0 / jnp.sum(x, axis=0, keepdims=True)) for x in weights]
        probs_b = [x.astype(jnp.bfloat16) for x in probs]
        out_t = [
            jnp.dot(values_t[:, :stop], x, preferred_element_type=jnp.float32).astype(jnp.bfloat16)
            for (_, _, stop), x in zip(items, probs_b)
        ]
        delta = [
            jnp.sum(
                d_t[h][:, start:stop].astype(jnp.float32) * x.astype(jnp.float32),
                axis=0,
                keepdims=True,
            )
            for (h, start, stop), x in zip(items, out_t)
        ]
        dscore = [
            (p * (x - t)).astype(jnp.bfloat16) for p, x, t in zip(probs, dprob, delta)
        ]
        dq_t = [
            (jnp.dot(keys_t[:, :stop], x, preferred_element_type=jnp.float32) * scale).astype(
                jnp.bfloat16
            )
            for (_, _, stop), x in zip(items, dscore)
        ]
        for (h, start, stop), x, p, o, q in zip(items, dscore, probs_b, out_t, dq_t):
            columns = slice(h * size, (h + 1) * size)
            dk_sum[:stop] += jnp.dot(x, qkv[start:stop, columns], preferred_element_type=jnp.float32)
            dv_sum[:stop] += jnp.dot(p, cot_ref[start:stop, columns], preferred_element_type=jnp.float32)
            out_ref[start:stop, columns] = o.T
            grad_ref[start:stop, columns] = q.T
    grad_ref[:, heads * size : (heads + 1) * size] = (dk_sum[...] * scale).astype(jnp.bfloat16)
    grad_ref[:, (heads + 1) * size : (heads + 2) * size] = dv_sum[...].astype(jnp.bfloat16)


def attend(place, segments, cotangent, group, arrived):
    slots, cols = arrived.shape
    size = HEAD_DIMENSION
    heads = cols // size - 2
    length = cotangent.shape[0]
    abreast = max(1, 5 * 512 * 512 // (length * length))
    return pl.pallas_call(
        functools.partial(attend_kernel, heads, 256, abreast),
        grid=(1,),
        out_shape=[
            jax.ShapeDtypeStruct((length, heads * size), jnp.bfloat16),
            jax.ShapeDtypeStruct((length, cols), jnp.bfloat16),
        ],
        in_specs=[VMEM, VMEM, VMEM, pl.BlockSpec((length, heads * size), lambda i: (0, group)), VMEM],
        out_specs=[VMEM, VMEM],
        scratch_shapes=[
            pltpu.VMEM((length, cols), jnp.bfloat16),
            pltpu.VMEM((length, length), jnp.float32),
            pltpu.VMEM((length, size), jnp.float32),
            pltpu.VMEM((length, size), jnp.float32),
        ],
        compiler_params=pltpu.CompilerParams(vmem_limit_bytes=VMEM_LIMIT),
        cost_estimate=pl.CostEstimate(
            flops=12 * heads * length * length * size + 2 * length * slots * cols,
            bytes_accessed=2 * (slots * cols + 3 * length * cols),
            transcendentals=heads * length * length,
        ),
        name="attend",
    )(place, segments[None, :], segments[:, None], cotangent, arrived)


def pack_kernel(n_seq, me_ref, slot_ref, spot_ref, *refs):
    own = refs[0]
    rows_a = refs[1:n_seq]
    rows_b = refs[n_seq : 2 * n_seq - 1]
    out_ref, rows_v, slots_v, sem = refs[2 * n_seq - 1 :]
    packs, _, total = slots_v.shape
    sets = slot_ref.shape[0] // n_seq
    span = slot_ref.shape[1]
    each = total // (n_seq * sets)
    odd, z = me_ref[0] & 1, me_ref[1]
    p = pl.program_id(0)
    across = (((1,), (1,)), ((), ()))

    @pl.when(p == 0)
    def _():
        copies = [
            line_copy(own, rows_a, rows_b, k, z, odd, lambda r: r, rows_v.at[k], sem.at[k])
            for k in range(n_seq)
        ]
        for start, _ in copies:
            start()
        order = lax.broadcasted_iota(jnp.int32, (packs * each, span), 0)
        for k in range(n_seq):
            copies[k][1]()
            for g in range(sets):
                at = k * sets + g
                pick = (order == slot_ref[at : at + 1, :]).astype(jnp.bfloat16)
                tok = rows_v.shape[3]
                pieces = [rows_v[k, i] for i in range(g * span // tok, (g + 1) * span // tok)]
                moved = lax.dot_general(
                    jnp.concatenate(pieces, axis=1),
                    pick,
                    across,
                    preferred_element_type=jnp.float32,
                ).astype(jnp.bfloat16)
                for q in range(packs):
                    slots_v[q, :, at * each : (at + 1) * each] = moved[:, q * each : (q + 1) * each]

    spots = lax.broadcasted_iota(jnp.int32, (out_ref.shape[1], total), 0)
    pick = (spots == spot_ref[pl.ds(p, 1), :]).astype(jnp.bfloat16)
    out_ref[...] = lax.dot_general(
        slots_v[p], pick, across, preferred_element_type=jnp.float32
    ).astype(jnp.bfloat16)


def pack_columns(place, slot, spot, own, rows_a, rows_b):
    packs, total = spot.shape
    n_fsdp, cols, tok = own.shape
    n_seq = len(rows_a) + 1
    tokens = n_seq * n_fsdp * tok
    length = tokens // packs
    return pl.pallas_call(
        functools.partial(pack_kernel, n_seq),
        grid=(packs,),
        out_shape=jax.ShapeDtypeStruct((cols, tokens), jnp.bfloat16),
        in_specs=[
            SMEM,
            pl.BlockSpec(slot.shape, lambda i: (0, 0)),
            pl.BlockSpec(spot.shape, lambda i: (0, 0)),
        ]
        + [ANY] * (2 * n_seq - 1),
        out_specs=pl.BlockSpec((cols, length), lambda i: (0, i)),
        scratch_shapes=[
            pltpu.VMEM((n_seq, n_fsdp, cols, tok), jnp.bfloat16),
            pltpu.VMEM((packs, cols, total), jnp.bfloat16),
            pltpu.SemaphoreType.DMA((n_seq,)),
        ],
        compiler_params=pltpu.CompilerParams(vmem_limit_bytes=VMEM_LIMIT),
        cost_estimate=pl.CostEstimate(
            flops=4 * packs * total * length * cols,
            bytes_accessed=4 * tokens * cols,
            transcendentals=0,
        ),
        name="pack_columns",
    )(place, slot, spot, own, *rows_a, *rows_b)


def grads_kernel(layout, group, adds, has_before, me_ref, packed_ref, *refs):
    count = sum(len(flips) for _, _, flips in layout)
    before = refs[count : count + 3]
    gq_ref, gk_ref, gv_ref, packed_v, d_v, acc, sem, sem_p, sem_o = refs[
        count + (3 if has_before else 0) :
    ]
    me = me_ref[0]
    steps, width, both = packed_v.shape
    length = both // 2
    cols = d_v.shape[2]
    size = HEAD_DIMENSION
    q_cols = cols - 2 * size

    def results(refs):
        return (
            (acc.at[:, pl.ds(0, q_cols)], refs[0].at[:, pl.ds(group * q_cols, q_cols)]),
            (acc.at[:, pl.ds(q_cols, size)], refs[1].at[:, pl.ds(group * size, size)]),
            (acc.at[:, pl.ds(q_cols + size, size)], refs[2].at[:, pl.ds(group * size, size)]),
        )

    copies = [[] for _ in range(steps)]
    at = 0
    for j, (mask, change, flips) in enumerate(layout):
        for flip in flips:
            start = pl.multiple_of(((me & 1) ^ flip) * length, length)
            copies[j].append(
                pltpu.make_async_copy(refs[at], d_v.at[j, pl.ds(start, length)], sem.at[at])
            )
            at += 1
        start = pl.multiple_of(((me >> 1) ^ (mask + change * (me & 1))) * both, both)
        copies[j].append(
            pltpu.make_async_copy(packed_ref.at[:, pl.ds(start, both)], packed_v.at[j], sem_p.at[j])
        )
    for j in range(min(2, steps)):
        for copy in copies[j]:
            copy.start()
    if adds:
        old = [pltpu.make_async_copy(r, a, sem_o.at[i]) for i, (a, r) in enumerate(results(before))]
        for copy in old:
            copy.start()
    for j in range(steps):
        for copy in copies[j]:
            copy.wait()
        if j + 2 < steps:
            for copy in copies[j + 2]:
                copy.start()
        part = jnp.dot(packed_v[j], d_v[j], preferred_element_type=jnp.float32)
        if j == 0 and adds:
            for copy in old:
                copy.wait()
        if j == 0 and not adds:
            acc[...] = part
        else:
            acc[...] += part
    outs = [
        pltpu.make_async_copy(a, r, sem_o.at[i])
        for i, (a, r) in enumerate(results((gq_ref, gk_ref, gv_ref)))
    ]
    for copy in outs:
        copy.start()
    for copy in outs:
        copy.wait()


def gradients(place, packed, chunks, group, groups, before, adds):
    layout = [(mask, change, [flip for flip, _ in parts]) for mask, change, parts in chunks]
    pieces = [part for _, _, parts in chunks for _, part in parts]
    width = packed.shape[0]
    length, cols = pieces[0].shape
    steps = len(chunks)
    size = HEAD_DIMENSION
    shapes = [
        jax.ShapeDtypeStruct((width, groups * (cols - 2 * size)), jnp.float32),
        jax.ShapeDtypeStruct((width, groups * size), jnp.float32),
        jax.ShapeDtypeStruct((width, groups * size), jnp.float32),
    ]
    extra = [] if before is None else list(before)
    return pl.pallas_call(
        functools.partial(grads_kernel, layout, group, adds, before is not None),
        out_shape=shapes,
        in_specs=[SMEM] + [ANY] * (1 + len(pieces) + len(extra)),
        out_specs=[ANY] * 3,
        input_output_aliases={2 + len(pieces) + i: i for i in range(len(extra))},
        scratch_shapes=[
            pltpu.VMEM((steps, width, 2 * length), jnp.bfloat16),
            pltpu.VMEM((steps, 2 * length, cols), jnp.bfloat16),
            pltpu.VMEM((width, cols), jnp.float32),
            pltpu.SemaphoreType.DMA((len(pieces),)),
            pltpu.SemaphoreType.DMA((steps,)),
            pltpu.SemaphoreType.DMA((3,)),
        ],
        compiler_params=pltpu.CompilerParams(vmem_limit_bytes=VMEM_LIMIT),
        cost_estimate=pl.CostEstimate(
            flops=4 * steps * length * width * cols,
            bytes_accessed=4 * steps * length * (width + cols) + 4 * width * cols,
            transcendentals=0,
        ),
        name="gradients",
    )(place, packed, *pieces, *extra)


def on_device(hidden, destination, segment_ids, cotangent, w_query, key_weight, value_weight):
    tok_rows, width = hidden.shape
    n_fsdp = lax.axis_size("fsdp")
    n_seq = lax.axis_size("seq")
    length = n_seq * tok_rows
    size = HEAD_DIMENSION
    groups = key_weight.shape[1] // size
    q_cols = w_query.shape[1] // groups
    cap = n_seq * n_seq * (2 * tok_rows // (n_fsdp * n_seq))
    f = lax.axis_index("fsdp")
    z = lax.axis_index("seq")
    here = jnp.stack([f, z]).astype(jnp.int32)

    block = jnp.concatenate(
        [
            part[:, g * part.shape[1] // groups : (g + 1) * part.shape[1] // groups]
            for g in range(groups)
            for part in (w_query, key_weight, value_weight)
        ],
        axis=1,
    )
    high = axis_bits(n_fsdp)
    rounds = len(high) == 2 and n_seq == 4 and groups == 2
    gather = gather_all_rounds if rounds else gather_all
    columns = jnp.transpose(hidden.reshape(tok_rows, n_fsdp, width // n_fsdp), (1, 2, 0))
    each = n_seq * (2 * tok_rows // (n_fsdp * n_seq))
    order = jnp.arange(tok_rows, dtype=jnp.int32)
    earlier = order[:, None] < order[None, :]

    def ranks(target):
        same = target[..., :, None] == target[..., None, :]
        return jnp.sum((same & earlier).astype(jnp.int32), axis=-2)

    def from_here(x, axis):
        return lax.dynamic_slice_in_dim(jnp.concatenate([x, x], axis), z, n_seq, axis)

    def index_of(dest):
        mine = lax.dynamic_index_in_dim(dest, f, 0, keepdims=False)
        target = mine // length
        slot = target * cap + jnp.arange(n_seq, dtype=jnp.int32)[:, None] * each + ranks(target)
        slot = from_here(slot, 0).reshape(1, length)
        target = dest // length
        slots = target * each + ranks(target)
        numbers = jnp.arange(n_fsdp * each, dtype=jnp.int32)
        hit = slots[:, :, None, :] == numbers[None, None, :, None]
        spots = jnp.sum(jnp.where(hit, (dest % length + 1)[:, :, None, :], 0), axis=-1) - 1
        span = 128 // each
        within = (jnp.arange(n_fsdp, dtype=jnp.int32) % span)[:, None, None]
        slots = target * (span * each - each) + within * each + slots
        spots = spots.reshape(n_fsdp, n_seq, n_fsdp, each)
        place = lax.dynamic_index_in_dim(spots, f, 2, keepdims=False).reshape(1, n_fsdp * cap)
        slots = jnp.swapaxes(from_here(slots, 1), 0, 1).reshape(-1, span * tok_rows)
        spots = jnp.transpose(from_here(spots, 1), (2, 1, 0, 3)).reshape(n_fsdp, -1)
        return slot, place, slots, spots

    weights, rows_a, rows_b, index, columns = gather(block, hidden, destination, columns, index_of)
    slot, place, slots, spots = index

    def grads_of(packed, parts, group, before, adds=False):
        return gradients(here, packed, parts, group, groups, before, adds)

    exchange = lambda x: lax.all_to_all(x, "fsdp", split_axis=0, concat_axis=0, tiled=True)
    if not rounds:
        sent = [
            project(here, slot, hidden, rows_a, rows_b, weights, cap, g, groups)
            for g in range(groups)
        ]
        results = [
            attend(place, segment_ids[0], cotangent, g, exchange(sent[g])) for g in range(groups)
        ]
        packed = pack_columns(here, slots, spots, columns, *line_gather(columns))
        grads = None
        for g in range(groups):
            grads = grads_of(packed, in_masks(spread(results[g][1], high + [1])), g, grads)
        outs = [out for out, _ in results]
        return (jnp.concatenate(outs, axis=1) if groups > 1 else outs[0], *grads)

    x, y = high
    a1, b1 = line_step(columns, columns)
    sent0 = project(here, slot, hidden, rows_a, rows_b, weights, cap, 0, 2)
    arrived0 = exchange(sent0)
    ((slot, a1, b1, _),) = together((slot, a1, b1, sent0))
    sent1 = project(here, slot, hidden, rows_a, rows_b, weights, cap, 1, 2)
    arrived1 = exchange(sent1)
    a2, b2 = line_step(a1, b1)
    out0, g0 = attend(place, segment_ids[0], cotangent, 0, after(arrived0, sent1))
    ((g0, a2, b2),) = together((g0, a2, b2))
    s0, n0 = swap(g0, "fsdp", 1), by_core(g0, x, y)
    a3, b3 = line_step(a2, b2)
    out1, g1 = attend(place, segment_ids[0], cotangent, 1, after(arrived1, g0))
    ((s0, n0, g1),) = together((s0, n0, g1))
    m0, n1, d0 = by_core(s0, x, y), by_core(g1, x, y), by_core(n0, y, x)
    packed = pack_columns(here, slots, spots, columns, [a1, a2, a3], [b1, b2, b3])
    ((packed, m0, n0, n1, d0, g1),) = together((packed, m0, n0, n1, d0, g1))
    s1 = swap(g1, "fsdp", 1)
    m1, d1 = by_core(s1, x, y), by_core(n1, y, x)
    f0 = [swap(n0, "fsdp", 1), swap(m0, "fsdp", 1)]
    e0 = swap(d0, "fsdp", 1)
    grads = grads_of(packed, in_pairs([g0, s0], [n0, m0], f0, [d0, e0]), 0, None)
    attn_out = jnp.concatenate([out0, out1], axis=1)
    ((m1, d1, n1, attn_out, *grads),) = together((m1, d1, n1, attn_out, *grads))
    f1 = [swap(n1, "fsdp", 1), swap(m1, "fsdp", 1)]
    e1 = swap(d1, "fsdp", 1)
    parts = in_pairs([g1, s1], [n1, m1], f1, [d1, e1])
    grads = grads_of(packed, parts[:2], 1, grads)
    grads = grads_of(packed, parts[2:], 1, grads, True)
    return (attn_out, *grads)


def solution(mesh):
    placed = (
        P(("fsdp", "seq"), None),
        P(("fsdp", "seq")),
        P("fsdp", None),
        P("fsdp", "seq"),
        P("fsdp", "seq"),
        P("fsdp", "seq"),
        P("fsdp", "seq"),
    )
    return jax.shard_map(
        on_device,
        mesh=mesh,
        in_specs=placed,
        out_specs=(P("fsdp", "seq"), P("fsdp", "seq"), P("fsdp", "seq"), P("fsdp", "seq")),
        check_vma=False,
    )
```
